256 devices in a mesh: frame: 64 (over x, y_hi, z), tensor: 4 (over y_lo, core).
Axes of the slice: x: 4, y: 4 (y_hi: 2, y_lo: 2; y = y_hi * 2 + y_lo), z: 8, core: 2. Of those that a mesh axis runs over, the one named last changes fastest.
Arguments:
- queries: bfloat16 [24576, 2560], P('frame', 'tensor'), may hold values from -320 to 320, as said below
- keys: bfloat16 [24576, 2560], P('frame', 'tensor'), may hold values from -12 to 12
- values: bfloat16 [24576, 2560], P('frame', 'tensor'), may hold values from -6 to 6
- stream_in: bfloat16 [24576, 5120], P('frame', 'tensor'), may hold values from -120 to 120
- out_weight: bfloat16 [2560, 5120], P('tensor'), may hold values from -0.5 to 0.5
- time_weight: bfloat16 [3, 256, 5120], P(None, None, 'tensor'), may hold values from -0.375 to 0.375
- head_weight: bfloat16 [5120, 64], P('tensor'), may hold values from -0.078125 to 0.078125
- latent: float32 [24576, 64], P('frame'), may hold values from -6 to 6
- new_noise: float32 [384, 64], replicated, may hold values from -6 to 6
- levels: int32 [64], P('frame'), may hold values from 1 to 128, as said below
- timesteps: int32 [129], replicated, may hold values from 0 to 1000, as said below
Outputs:
- stream: bfloat16 [24576, 5120], P('frame', 'tensor')
- velocity: float32 [24576, 64], P('frame')
- queue_next: float32 [24576, 64], P('frame')
The draws below stay inside these ranges and needn't reach their ends.
Inputs may be any that keep to these rules, and one draw needn't show every extreme that they name: `queries`: queries of the hidden draw may reach large magnitudes. `levels`: Non-decreasing along the queue; the first slot holds level 1 and the last slot level 128. `timesteps`: strictly rising; the first entry is 0 and the last is 1000.
All inputs are finite; a program needn't handle non-finite values.
Results may differ from the reference program's by a relative error of at most 0.013.
Values may be sent and summed in bfloat16 or wider, within the bound.
No kernel may reach another device: no remote copies, remote signals or barrier semaphores. Data moves between devices by JAX's collectives and lax.ppermute only.
A program may use at most 128 MiB of HBM per device.

```python
import math
import jax
import jax.numpy as jnp
from jax import lax

D = 5120
HEADS = 20
HD = 128
CL = 64
TFREQ = 256
TOK = 384
PART = 8
FRAMES = 64
LEVELS = 128
HH = 2560
N_TENSOR = 4


def query_key_base(key):
    first_key, second_key = jax.random.split(jax.random.fold_in(key, 101))
    shape = (FRAMES * TOK, HEADS * HD)
    base_queries = 1.4 * jnp.clip(jax.random.normal(first_key, shape, jnp.float32), -8.0, 8.0)
    base_keys = 1.4 * jnp.clip(jax.random.normal(second_key, shape, jnp.float32), -8.0, 8.0)
    return (base_queries, base_keys)


def draw_queries(key, part):
    base_queries, base_keys = query_key_base(key)
    return base_queries.astype(jnp.bfloat16)


def draw_keys(key, part):
    base_queries, base_keys = query_key_base(key)
    return base_keys.astype(jnp.bfloat16)


def draw_stream_in(key, part):
    key = jax.random.fold_in(key, 5)
    first_key = jax.random.fold_in(key, 0)
    column_scale = 3.0 ** (jnp.arange(D, dtype=jnp.float32) / D)
    base_values = jnp.clip(jax.random.normal(first_key, (FRAMES * TOK, D), jnp.float32), -5.0, 5.0) * column_scale[None, :]
    return base_values.astype(jnp.bfloat16)


def draw_levels(key, part):
    key = jax.random.fold_in(key, 7)
    drawn = jnp.sort(jax.random.randint(key, (FRAMES,), 1, LEVELS + 1, dtype=jnp.int32))
    drawn = drawn.at[0].set(1)
    drawn = drawn.at[FRAMES - 1].set(LEVELS)
    return drawn.astype(jnp.int32)


def draw_timesteps(key, part):
    key = jax.random.fold_in(key, 9)
    increments = jax.random.randint(key, (LEVELS - 1,), 1, 1000 // LEVELS + 1, dtype=jnp.int32)
    rising = jnp.cumsum(increments).astype(jnp.int32)
    return jnp.concatenate([jnp.zeros((1,), jnp.int32), rising, jnp.full((1,), 1000, jnp.int32)]).astype(jnp.int32)


def block_scale(stream_key, extent, cuts, low, high):
    loudness = 1.0
    for axis_at, shards_of in cuts:
        draws = jax.random.uniform(jax.random.fold_in(jax.random.fold_in(stream_key, 6), axis_at), (shards_of,), jnp.float32, low / len(cuts), high / len(cuts))
        loudness = loudness * jnp.repeat(jnp.exp(draws), extent[axis_at] // shards_of).reshape((-1,) + (1,) * (len(extent) - 1 - axis_at))
    return loudness


def bell_draw(stream_key, shape, scale, limit, cuts=(), kind=jnp.bfloat16):
    values = jax.random.normal(stream_key, shape, jnp.float32) * scale
    if len(cuts) > 0:
        values = block_scale(stream_key, shape, cuts, -0.22, 0.18) * values
    return jnp.clip(values, min=-limit, max=limit).astype(kind)


def setup_inputs(seed: int = 0) -> dict:
    key_list = jax.random.split(jax.random.key(seed), 12)
    queries = draw_queries(jax.random.fold_in(key_list[11], 71), 0)
    keys = draw_keys(jax.random.fold_in(key_list[11], 71), 0)
    values = bell_draw(key_list[2], (FRAMES * TOK, HH), 1.0, 6.0, ((0, 64), (1, 4)))
    stream_in = draw_stream_in(jax.random.fold_in(key_list[11], 71), 0)
    out_weight = bell_draw(key_list[4], (HH, D), (HH // 16) ** -0.5, 0.5, ((0, 4),))
    time_weight = bell_draw(key_list[5], (3, TFREQ, D), TFREQ ** -0.5, 0.375, ((2, 4),))
    head_weight = bell_draw(key_list[6], (D, CL), D ** -0.5, 0.078125, ((0, 4),))
    latent = bell_draw(key_list[7], (FRAMES * TOK, CL), 1.0, 6.0, ((0, 64),), jnp.float32)
    new_noise = bell_draw(key_list[8], (TOK, CL), 1.0, 6.0, (), jnp.float32)
    levels = draw_levels(jax.random.fold_in(key_list[11], 71), 0)
    timesteps = draw_timesteps(jax.random.fold_in(key_list[11], 71), 0)
    return dict(queries=queries, keys=keys, values=values, stream_in=stream_in, out_weight=out_weight, time_weight=time_weight, head_weight=head_weight, latent=latent, new_noise=new_noise, levels=levels, timesteps=timesteps)


def sinusoid(time_values, freq_width):
    half_width = freq_width // 2
    frequencies = jnp.exp(-math.log(10000.0) * jnp.arange(half_width, dtype=jnp.float32) / half_width)
    angles = time_values[:, None] * frequencies[None, :]
    return jnp.concatenate([jnp.cos(angles), jnp.sin(angles)], axis=-1)

def attend_all(packed):
    query_rows, key_rows, value_rows = packed
    scores = jnp.dot(query_rows, key_rows.T, preferred_element_type=jnp.float32) * HD ** (-0.5)
    peaks = lax.optimization_barrier(jnp.max(scores, axis=1, keepdims=True))
    weights = jnp.exp(scores - peaks)
    totals = lax.optimization_barrier(jnp.sum(weights, axis=1, keepdims=True))
    mixed_rows = jnp.dot(weights.astype(jnp.bfloat16), value_rows, preferred_element_type=jnp.float32)
    return (mixed_rows / totals).astype(jnp.bfloat16)

def reference(queries, keys, values, stream_in, out_weight, time_weight, head_weight, latent, new_noise, levels, timesteps):
    t_now = timesteps[levels].astype(jnp.float32)
    t_next = timesteps[levels - 1].astype(jnp.float32)
    embedding = sinusoid(t_now, TFREQ).astype(jnp.bfloat16)
    modulation = jnp.einsum('fj,cjd->cfd', embedding.astype(jnp.float32), time_weight.astype(jnp.float32), precision=lax.Precision.HIGHEST)
    group_count = FRAMES // PART
    span_rows = PART * TOK

    def to_heads(array):
        return array.reshape(group_count, span_rows, HEADS, HD).transpose(0, 2, 1, 3).reshape(group_count * HEADS, span_rows, HD)
    attended = lax.map(attend_all, (to_heads(queries), to_heads(keys), to_heads(values)))
    attended = attended.reshape(group_count, HEADS, span_rows, HD).transpose(0, 2, 1, 3).reshape(FRAMES * TOK, HEADS * HD)
    group_width = HEADS * HD // N_TENSOR
    mixed_sum = jnp.zeros((FRAMES * TOK, D), jnp.float32)
    for group_index in range(N_TENSOR):
        low = group_index * group_width
        partial_term = jnp.dot(attended[:, low:low + group_width], out_weight[low:low + group_width], preferred_element_type=jnp.float32).astype(jnp.bfloat16)
        partial_term = lax.optimization_barrier(partial_term)
        mixed_sum = mixed_sum + partial_term.astype(jnp.float32)
    hidden = stream_in.astype(jnp.float32).reshape(FRAMES, TOK, D) + modulation[0][:, None, :] * mixed_sum.reshape(FRAMES, TOK, D)
    stream = hidden.reshape(FRAMES * TOK, D).astype(jnp.bfloat16)
    row_mean = lax.optimization_barrier(jnp.mean(hidden, axis=2, keepdims=True))
    row_var = lax.optimization_barrier(jnp.mean(hidden * hidden, axis=2, keepdims=True)) - row_mean * row_mean
    normed = (hidden - row_mean) * lax.rsqrt(row_var + 1e-06) * (1.0 + modulation[2][:, None, :]) + modulation[1][:, None, :]
    velocity = jnp.dot(normed.reshape(FRAMES * TOK, D), head_weight.astype(jnp.float32), precision=lax.Precision.HIGHEST)
    step_size = (t_next - t_now) / 1000.0
    updated = latent.reshape(FRAMES, TOK, CL) + step_size[:, None, None] * velocity.reshape(FRAMES, TOK, CL)
    queue_next = jnp.concatenate([updated[1:].reshape((FRAMES - 1) * TOK, CL), new_noise], axis=0)
    return (stream, velocity, queue_next)
```

```python
import math

import jax
import jax.numpy as jnp
from jax import lax
from jax.experimental import pallas as pl
from jax.experimental.pallas import tpu as pltpu
from jax.sharding import PartitionSpec as P

D = 5120
HD = 128
TFREQ = 256
PART = 8
N_TENSOR = 4
F32 = jnp.float32
BF16 = jnp.bfloat16
ROW_BLOCK = 128
CHUNKS = ((0, 3), (3, 2))
EXP_SCALE = HD ** (-0.5) / math.log(2.0)
VMEM_LIMIT = 40 * 1024 * 1024


def params():
    return pltpu.CompilerParams(vmem_limit_bytes=VMEM_LIMIT)


def ring(x, by):
    size = lax.axis_size("frame")
    pairs = [(i, i // PART * PART + (i + by) % PART) for i in range(size)]
    return lax.ppermute(x, "frame", pairs)


def peer(x, mask):
    return lax.ppermute(x, "tensor", [(i, i ^ mask) for i in range(N_TENSOR)])


def shifted(x, axis, by):
    length = lax.axis_size(axis)
    pairs = [(i, i + by) for i in range(length) if 0 <= i + by < length]
    return lax.ppermute(x, axis, pairs)


def sinusoid(time_values, freq_width):
    half_width = freq_width // 2
    frequencies = jnp.exp(
        -math.log(10000.0) * jnp.arange(half_width, dtype=jnp.float32) / half_width
    )
    angles = time_values[:, None] * frequencies[None, :]
    return jnp.concatenate([jnp.cos(angles), jnp.sin(angles)], axis=-1)


def lookup(table_values, positions):
    matches = jnp.arange(table_values.shape[0], dtype=jnp.int32)[None, :] == positions[:, None]
    return jnp.sum(jnp.where(matches, table_values[None, :], 0), axis=1).astype(jnp.float32)


def dot(a, b):
    return jnp.dot(a, b, preferred_element_type=F32)


def dot_t(a, b):
    return lax.dot_general(a, b, (((1,), (1,)), ((), ())), preferred_element_type=F32)


def split3(x):
    hi = x.astype(BF16)
    rest = x - hi.astype(F32)
    mid = rest.astype(BF16)
    return hi, mid, (rest - mid.astype(F32)).astype(BF16)


def join3(x):
    x = x.astype(F32)
    return x[0] + x[1] + x[2]


def attend_kernel(head_low, head_count, block_count, first, last, split_kv, *refs):
    refs = list(refs)
    q_ref = refs.pop(0)
    width = head_count * HD
    blocks = []
    for _ in range(block_count):
        if split_kv:
            k_ref, v_ref = refs.pop(0), refs.pop(0)
            blocks.append((k_ref, 0, v_ref, 0))
        else:
            kv_ref = refs.pop(0)
            blocks.append((kv_ref, 0, kv_ref, width))
    if not first:
        acc_in, peak_in, total_in = refs.pop(0), refs.pop(0), refs.pop(0)
    for head in range(head_count):
        low = head * HD
        for row in range(0, q_ref.shape[0], ROW_BLOCK):
            rows = slice(row, row + ROW_BLOCK)
            lanes = slice(low, low + HD)
            query = q_ref[rows, (head_low + head) * HD : (head_low + head + 1) * HD]
            scores = [
                dot_t(query, k_ref[:, k_at + low : k_at + low + HD])
                for k_ref, k_at, _, _ in blocks
            ]
            peak = max_of([jnp.max(s, axis=1, keepdims=True) for s in scores])
            if not first:
                old_peak = peak_in[rows, low : low + 1]
                peak = jnp.maximum(peak, old_peak)
            acc = None
            total = None
            for s, (_, _, v_ref, v_at) in zip(scores, blocks):
                weights = jnp.exp2((s - peak) * EXP_SCALE)
                part = sum_lanes(weights)
                total = part if total is None else total + part
                mixed = dot(weights.astype(BF16), v_ref[:, v_at + low : v_at + low + HD])
                acc = mixed if acc is None else acc + mixed
            if not first:
                shrink = jnp.exp2((old_peak - peak) * EXP_SCALE)
                acc = acc + acc_in[rows, lanes] * shrink
                total = total + total_in[rows, lanes] * shrink
            if last:
                denominator = jnp.sum(total, axis=1, keepdims=True)
                refs[0][rows, lanes] = (acc / denominator).astype(BF16)
            else:
                refs[0][rows, lanes] = acc
                refs[1][rows, lanes] = jnp.broadcast_to(peak, acc.shape)
                refs[2][rows, lanes] = total


def max_of(values):
    result = values[0]
    for value in values[1:]:
        result = jnp.maximum(result, value)
    return result


def sum_lanes(x):
    result = x[:, :HD]
    for low in range(HD, x.shape[1], HD):
        result = result + x[:, low : low + HD]
    return result


def attend(queries, chunk, blocks, state, last, split_kv=False):
    head_low, head_count = chunk
    row_count = queries.shape[0]
    width = head_count * HD
    operands = [queries]
    for block in blocks:
        operands += list(block) if split_kv else [block]
    first = state is None
    if not first:
        operands += list(state)
    if last:
        out_shape = jax.ShapeDtypeStruct((row_count, width), BF16)
    else:
        out_shape = [jax.ShapeDtypeStruct((row_count, width), F32)] * 3
    units = head_count * len(blocks)

    def body(*refs):
        attend_kernel(head_low, head_count, len(blocks), first, last, split_kv, *refs)

    return pl.pallas_call(
        body,
        out_shape=out_shape,
        compiler_params=params(),
        cost_estimate=pl.CostEstimate(
            flops=units * 4 * row_count * row_count * HD * 3,
            bytes_accessed=units * 4 * row_count * HD,
            transcendentals=units * row_count * row_count,
        ),
    )(*operands)


def modulate_kernel(embedding_ref, time_ref, head_ref, mod_ref, extra_ref):
    width = mod_ref.shape[1]
    embedding = jnp.broadcast_to(embedding_ref[...], (16, TFREQ))
    gate = dot(embedding, time_ref[0])[:1]
    shift = dot(embedding, time_ref[1])[:1]
    lift = 1.0 + dot(embedding, time_ref[2])[:1]
    mod_ref[...] = jnp.concatenate([gate, shift, lift, jnp.zeros((5, width), F32)], axis=0)
    pieces = split3(lift) + split3(shift)
    stacked = jnp.concatenate([x.astype(F32) for x in pieces] + [jnp.zeros((10, width), F32)], axis=0)
    products = dot(stacked.astype(BF16), head_ref[...])
    lift_head = products[0:1] + products[1:2] + products[2:3]
    shift_head = products[3:4] + products[4:5] + products[5:6]
    rows = [x.astype(F32) for x in split3(lift_head) + split3(shift_head)]
    rows = jnp.concatenate(rows + [jnp.zeros((10, rows[0].shape[1]), F32)], axis=0)
    extra_ref[...] = jnp.concatenate([rows, jnp.zeros_like(rows)], axis=1).astype(BF16)


def project_kernel(a0, a1, a2, a3, w0, w1, w2, w3, out_ref):
    depth = a0.shape[1]
    for row in range(0, out_ref.shape[0], ROW_BLOCK):
        rows = slice(row, row + ROW_BLOCK)
        acc = None
        for a_ref, w_ref in ((a0, w0), (a1, w1), (a2, w2), (a3, w3)):
            part = dot(a_ref[rows, :], w_ref[0:depth, :])
            acc = part if acc is None else acc + part
        out_ref[rows, :] = acc


def hidden_kernel(
    a0, a1, a2, a3, w0, w1, w2, w3, acc_ref, in_ref, mod_ref, head_ref, extra_ref, stream_ref, message_ref
):
    depth = a0.shape[1]
    low = w0.shape[0] - depth
    width = stream_ref.shape[1]
    row_count = stream_ref.shape[0]
    gate = mod_ref[0:1, :]
    lift = mod_ref[2:3, :]
    head = head_ref[...]
    for row in range(0, row_count, ROW_BLOCK):
        rows = slice(row, row + ROW_BLOCK)
        mixed = acc_ref[rows, :]
        for a_ref, w_ref in ((a0, w0), (a1, w1), (a2, w2), (a3, w3)):
            mixed = mixed + dot(a_ref[rows, :], w_ref[low:, :])
        hidden = in_ref[rows, :].astype(F32) + gate * mixed
        stream_ref[rows, :] = hidden.astype(BF16)
        mean = jnp.sum(hidden, axis=1, keepdims=True) * (1.0 / width)
        centered = hidden - mean
        spread = jnp.sum(centered * centered, axis=1, keepdims=True)
        lifted = centered * lift
        lifted_hi = lifted.astype(BF16)
        lifted_lo = (lifted - lifted_hi.astype(F32)).astype(BF16)
        share = dot(lifted_hi, head) + dot(lifted_lo, head)
        lane = lax.broadcasted_iota(jnp.int32, (ROW_BLOCK, share.shape[1]), 1)
        stats = jnp.zeros(lane.shape, F32)
        for at, piece in enumerate(split3(mean) + split3(spread)):
            stats = jnp.where(lane == at, piece.astype(F32), stats)
        message_ref[rows, :] = jnp.concatenate([share, stats], axis=1).astype(BF16)
    message_ref[row_count:, :] = extra_ref[...]


def finish_kernel(m0, m1, m2, m3, latent_ref, step_ref, velocity_ref, updated_ref):
    row_count, width = velocity_ref.shape
    refs = (m0, m1, m2, m3)

    def tree(values):
        return (values[0] + values[1]) + (values[2] + values[3])

    messages = [ref[0:row_count, :].astype(F32) for ref in refs]
    extras = [ref[row_count:, :].astype(F32) for ref in refs]
    shares = [m[:, :width] for m in messages]
    means = [m[:, width : width + 1] + m[:, width + 1 : width + 2] + m[:, width + 2 : width + 3] for m in messages]
    spreads = [
        m[:, width + 3 : width + 4] + m[:, width + 4 : width + 5] + m[:, width + 5 : width + 6]
        for m in messages
    ]
    lifts = [e[0:1, :width] + e[1:2, :width] + e[2:3, :width] for e in extras]
    shifts = [e[3:4, :width] + e[4:5, :width] + e[5:6, :width] for e in extras]
    mean = tree(means) * (1.0 / N_TENSOR)
    offsets = [x - mean for x in means]
    variance = tree(spreads) * (1.0 / D) + tree([x * x for x in offsets]) * (1.0 / N_TENSOR)
    inv_std = lax.rsqrt(variance + 1e-06)
    total = tree([s + o * b for s, o, b in zip(shares, offsets, lifts)])
    velocity = total * inv_std + tree(shifts)
    velocity_ref[...] = velocity
    updated_ref[...] = (latent_ref[...] + step_ref[0, 0] * velocity).astype(BF16)


def local(
    queries,
    keys,
    values,
    stream_in,
    out_weight,
    time_weight,
    head_weight,
    latent,
    new_noise,
    levels,
    timesteps,
):
    row_count, width = stream_in.shape
    frame_index = lax.axis_index("frame")
    frame_count = lax.axis_size("frame")
    tensor_index = lax.axis_index("tensor")

    gathered = []
    for low, count in CHUNKS:
        lanes = slice(low * HD, (low + count) * HD)
        gathered.append([jnp.concatenate([keys[:, lanes], values[:, lanes]], axis=1)])
    right = [g[0] for g in gathered]
    left = [g[0] for g in gathered]
    far = [None, None]
    for hop in range(4):
        for at, (_, count) in enumerate(CHUNKS):
            if hop < 3:
                right[at] = ring(right[at], 1)
                left[at] = ring(left[at], -1)
                gathered[at] += [right[at], left[at]]
            else:
                far[at] = (
                    ring(right[at][:, : count * HD], 1),
                    ring(left[at][:, count * HD :], -1),
                )

    def columns(mask):
        return lax.dynamic_slice(
            out_weight, (0, (tensor_index ^ mask) * width), (out_weight.shape[0], width)
        )

    own_weight = columns(0)
    weights = [own_weight] + [peer(columns(mask), mask) for mask in (1, 2, 3)]

    t_now = lookup(timesteps, levels)
    t_next = lookup(timesteps, levels - 1)
    embedding = sinusoid(t_now, TFREQ).astype(BF16)
    step = ((t_next - t_now) / 1000.0).reshape(1, 1)
    mod, extra = pl.pallas_call(
        modulate_kernel,
        out_shape=[jax.ShapeDtypeStruct((8, width), F32), jax.ShapeDtypeStruct((16, 128), BF16)],
        compiler_params=params(),
    )(embedding, time_weight, head_weight)

    attended = []
    for at, chunk in enumerate(CHUNKS):
        state = attend(queries, chunk, gathered[at][:3], None, False)
        state = attend(queries, chunk, gathered[at][3:5], state, False)
        state = attend(queries, chunk, gathered[at][5:7], state, False)
        mixed = attend(queries, chunk, [far[at]], state, True, split_kv=True)
        attended.append([mixed] + [peer(mixed, mask) for mask in (1, 2, 3)])

    first_part = pl.pallas_call(
        project_kernel,
        out_shape=jax.ShapeDtypeStruct((row_count, width), F32),
        compiler_params=params(),
        cost_estimate=pl.CostEstimate(
            flops=2 * row_count * 1536 * width, bytes_accessed=8 * 1024 * 1024, transcendentals=0
        ),
    )(*attended[0], *weights)
    stream, message = pl.pallas_call(
        hidden_kernel,
        out_shape=[
            jax.ShapeDtypeStruct((row_count, width), BF16),
            jax.ShapeDtypeStruct((row_count + 16, 128), BF16),
        ],
        compiler_params=params(),
    )(*attended[1], *weights, first_part, stream_in, mod, head_weight, extra)
    messages = [message] + [peer(message, mask) for mask in (1, 2, 3)]
    velocity, updated = pl.pallas_call(
        finish_kernel,
        in_specs=[pl.BlockSpec(memory_space=pltpu.VMEM)] * 5 + [pl.BlockSpec(memory_space=pltpu.SMEM)],
        out_shape=[
            jax.ShapeDtypeStruct(latent.shape, F32),
            jax.ShapeDtypeStruct(latent.shape, BF16),
        ],
        compiler_params=params(),
    )(*messages, latent, step)
    arrived = shifted(updated, "frame", -1).astype(F32)
    queue_next = jnp.where(frame_index == frame_count - 1, new_noise, arrived)
    return (stream, velocity, queue_next)


def solution(mesh):
    return jax.shard_map(
        local,
        mesh=mesh,
        in_specs=(
            P("frame", "tensor"),
            P("frame", "tensor"),
            P("frame", "tensor"),
            P("frame", "tensor"),
            P("tensor", None),
            P(None, None, "tensor"),
            P("tensor", None),
            P("frame", None),
            P(),
            P("frame"),
            P(),
        ),
        out_specs=(P("frame", "tensor"), P("frame", None), P("frame", None)),
        check_vma=False,
    )
```

```python
import math

import jax
import jax.numpy as jnp
from jax import lax
from jax.experimental import pallas as pl
from jax.experimental.pallas import tpu as pltpu
from jax.sharding import PartitionSpec as P

D = 5120
HD = 128
TFREQ = 256
PART = 8
N_TENSOR = 4
F32 = jnp.float32
BF16 = jnp.bfloat16
COLUMN_BLOCK = 256
SPREAD_HEADS = 4
HALF_STRIDE = 16
SMALL = pl.CostEstimate(flops=1000, bytes_accessed=1000, transcendentals=0)
EXP_SCALE = HD ** (-0.5) / math.log(2.0)
VMEM_LIMIT = 16 * 1024 * 1024


def params():
    return pltpu.CompilerParams(vmem_limit_bytes=VMEM_LIMIT)


def spread(x, distance, backward=False):
    pairs = []
    for frame in range(lax.axis_size("frame")):
        for core in range(N_TENSOR):
            at = (frame - core) % PART
            step = distance if (at + distance) % 2 == 0 else -distance
            target = frame // PART * PART + (frame + step) % PART
            pairs.append((frame * N_TENSOR + core, target * N_TENSOR + core))
    if backward:
        pairs = [(b, a) for a, b in pairs]
    return lax.ppermute(x, ("frame", "tensor"), pairs)


def swap_pair(x):
    pairs = []
    for frame in range(lax.axis_size("frame")):
        for core in range(N_TENSOR):
            at = (frame - core) % PART
            target = frame // PART * PART + ((at ^ 1) + core) % PART
            pairs.append((frame * N_TENSOR + core, target * N_TENSOR + core))
    return lax.ppermute(x, ("frame", "tensor"), pairs)


def swap_half(x):
    return lax.ppermute(x, "frame", [(i, i ^ HALF_STRIDE) for i in range(lax.axis_size("frame"))])


def peer(x, mask):
    return lax.ppermute(x, "tensor", [(i, i ^ mask) for i in range(N_TENSOR)])


def shifted(x, axis, by):
    length = lax.axis_size(axis)
    pairs = [(i, i + by) for i in range(length) if 0 <= i + by < length]
    return lax.ppermute(x, axis, pairs)


def sinusoid(time_values, freq_width):
    half_width = freq_width // 2
    frequencies = jnp.exp(
        -math.log(10000.0) * jnp.arange(half_width, dtype=jnp.float32) / half_width
    )
    angles = time_values[:, None] * frequencies[None, :]
    return jnp.concatenate([jnp.cos(angles), jnp.sin(angles)], axis=-1)


def lookup(table_values, positions):
    matches = jnp.arange(table_values.shape[0], dtype=jnp.int32)[None, :] == positions[:, None]
    return jnp.sum(jnp.where(matches, table_values[None, :], 0), axis=1).astype(jnp.float32)


def dot(a, b):
    return jnp.dot(a, b, preferred_element_type=F32)


def dot_t(a, b):
    return lax.dot_general(a, b, (((1,), (1,)), ((), ())), preferred_element_type=F32)


def split3(x):
    hi = x.astype(BF16)
    rest = x - hi.astype(F32)
    mid = rest.astype(BF16)
    return hi, mid, (rest - mid.astype(F32)).astype(BF16)


def pack_kernel(head_ref, q_ref, k_ref, v_ref, x1_ref, x2_ref, x3_ref, kv_ref, q_out_ref, sem):
    common = pl.ds(SPREAD_HEADS * HD, HD)

    def lanes(at):
        return pl.ds(pl.multiple_of(head_ref[at] * HD, HD), HD)

    copies = []

    def move(source, source_lanes, target, slot):
        copy = pltpu.make_async_copy(
            source.at[:, source_lanes], target.at[:, pl.ds(slot * HD, HD)], sem.at[len(copies)]
        )
        copy.start()
        copies.append(copy)

    for at, ref in ((3, x3_ref), (2, x2_ref), (1, x1_ref), (0, kv_ref)):
        move(k_ref, lanes(at), ref, 0)
        move(v_ref, lanes(at), ref, 1)
        move(k_ref, common, ref, 2)
        move(v_ref, common, ref, 3)
        if at:
            move(q_ref, lanes(at), ref, 4)
    move(q_ref, lanes(0), q_out_ref, 0)
    move(q_ref, common, q_out_ref, 1)
    for copy in copies:
        copy.wait()


def attend_kernel(query_lanes, own_query, block_count, state_low, first, last, *refs):
    refs = list(refs)
    q_refs = [refs.pop(0) for _ in query_lanes]
    blocks = [refs.pop(0) for _ in range(block_count)]
    if not first:
        acc_in, peak_in, total_in = refs.pop(0), refs.pop(0), refs.pop(0)
    row_count = q_refs[0].shape[0]
    for at, (q_ref, (q_low, shared)) in enumerate(zip(q_refs, query_lanes)):
        key_low = 2 * HD if shared else 0
        query = q_ref[:, q_low : q_low + HD]
        scores = [dot_t(query, ref[:, key_low : key_low + HD]) for ref in blocks]
        peak = max_of([jnp.max(s, axis=1, keepdims=True) for s in scores])
        rows = slice((state_low + at) * row_count, (state_low + at + 1) * row_count)
        if not first:
            old_peak = peak_in[rows, 0:1]
            peak = jnp.maximum(peak, old_peak)
        acc = None
        total = None
        for s, ref in zip(scores, blocks):
            weights = jnp.exp2((s - peak) * EXP_SCALE)
            part = sum_lanes(weights)
            total = part if total is None else total + part
            mixed = dot(weights.astype(BF16), ref[:, key_low + HD : key_low + 2 * HD])
            acc = mixed if acc is None else acc + mixed
        if not first:
            shrink = jnp.exp2((old_peak - peak) * EXP_SCALE)
            acc = acc + acc_in[rows, :] * shrink
            total = total + total_in[rows, :] * shrink
        if last:
            out = (acc / jnp.sum(total, axis=1, keepdims=True)).astype(BF16)
            if own_query:
                refs[0][:, at * HD : (at + 1) * HD] = out
            else:
                refs[at][...] = out
        else:
            refs[0][rows, :] = acc
            refs[1][rows, :] = jnp.broadcast_to(peak, acc.shape)
            refs[2][rows, :] = total


def max_of(values):
    result = values[0]
    for value in values[1:]:
        result = jnp.maximum(result, value)
    return result


def sum_lanes(x):
    result = x[:, :HD]
    for low in range(HD, x.shape[1], HD):
        result = result + x[:, low : low + HD]
    return result


def attend(queries, query_lanes, blocks, state, state_low, last, own_query):
    row_count = queries[0].shape[0]
    operands = list(queries) + list(blocks)
    first = state is None
    if not first:
        operands += list(state)
    if not last:
        out_shape = [jax.ShapeDtypeStruct((row_count * len(queries), HD), F32)] * 3
    elif own_query:
        out_shape = jax.ShapeDtypeStruct((row_count, HD * len(queries)), BF16)
    else:
        out_shape = [jax.ShapeDtypeStruct((row_count, HD), BF16)] * len(queries)

    def body(*refs):
        attend_kernel(query_lanes, own_query, len(blocks), state_low, first, last, *refs)

    return pl.pallas_call(body, out_shape=out_shape, compiler_params=params(), cost_estimate=SMALL)(*operands)


def modulate_kernel(embedding_ref, time_ref, head_ref, gate_ref, lifted_ref, extra_ref):
    width = gate_ref.shape[1]
    channels = head_ref.shape[0]
    embedding = jnp.broadcast_to(embedding_ref[...], (16, TFREQ))
    gate_ref[...] = dot(embedding, time_ref[0])[:8]
    shift = dot(embedding, time_ref[1])[:1]
    lift = 1.0 + dot(embedding, time_ref[2])[:1]
    head = head_ref[...].astype(F32)
    lifted = head * lift
    high = lifted.astype(BF16)
    low = (lifted - high.astype(F32)).astype(BF16)
    lifted_ref[0:channels] = high
    lifted_ref[channels:] = low
    lift_head = jnp.sum(high.astype(F32) + low.astype(F32), axis=1, keepdims=True)
    shift_head = jnp.sum(head * shift, axis=1, keepdims=True)
    extra_ref[...] = place(split3(lift_head) + split3(shift_head), extra_ref.shape).astype(BF16)


def place(pieces, shape):
    lane = lax.broadcasted_iota(jnp.int32, shape, 1)
    result = jnp.zeros(shape, F32)
    for at, piece in enumerate(pieces):
        result = jnp.where(lane == at, piece.astype(F32), result)
    return result


def head_rows(head_ref, w_ref, rows, lanes):
    parts = []
    for row in rows:
        if row is None:
            parts.append(w_ref[SPREAD_HEADS * HD : (SPREAD_HEADS + 1) * HD, lanes])
        else:
            parts.append(w_ref[pl.ds(pl.multiple_of(head_ref[row] * HD, HD), HD), lanes])
    return jnp.concatenate(parts, axis=0)


def column_blocks(width):
    return [(low, min(COLUMN_BLOCK, width - low)) for low in range(0, width, COLUMN_BLOCK)]


def project_kernel(halves, row_sets, with_base, head_ref, *refs):
    count = len(row_sets)
    out_ref = refs[-1]
    width = out_ref.shape[1]
    inputs, weights = refs[:count], refs[count : (1 + halves) * count]
    base_ref = refs[(1 + halves) * count] if with_base else None
    for half in range(halves):
        offset = 0
        if halves > 1:
            offset = pl.multiple_of((head_ref[8] ^ half) * (width // halves), HD)
        for low, size in column_blocks(width // halves):
            out_lanes = pl.ds(offset + low, size)
            acc = base_ref[:, out_lanes] if with_base else None
            for at, (a_ref, rows) in enumerate(zip(inputs, row_sets)):
                w_ref = weights[at * halves + half]
                part = dot(a_ref[...], head_rows(head_ref, w_ref, rows, pl.ds(low, size)))
                acc = part if acc is None else acc + part
            out_ref[:, out_lanes] = acc


def project(heads, inputs, weights, row_sets, base=None):
    row_count = inputs[0].shape[0]
    halves = len(weights) // len(inputs)
    width = weights[0].shape[1] * halves
    operands = [heads, *inputs, *weights] + ([] if base is None else [base])

    def body(*refs):
        project_kernel(halves, row_sets, base is not None, *refs)

    return pl.pallas_call(
        body,
        in_specs=[pl.BlockSpec(memory_space=pltpu.SMEM)]
        + [pl.BlockSpec(memory_space=pltpu.VMEM)] * (len(operands) - 1),
        out_shape=jax.ShapeDtypeStruct((row_count, width), F32),
        compiler_params=params(),
        cost_estimate=SMALL,
    )(*operands)


def hidden_kernel(
    row_sets,
    head_ref,
    a0,
    a1,
    w0_mine,
    w0_other,
    w1_mine,
    w1_other,
    acc_ref,
    in_ref,
    gate_ref,
    lifted_ref,
    extra_ref,
    stream_ref,
    message_ref,
):
    row_count, width = stream_ref.shape
    channels = extra_ref.shape[0]
    total = None
    squares = None
    share = None
    rest = None
    for half, low, size in [(h, *block) for h in range(2) for block in column_blocks(width // 2)]:
        lanes = pl.ds(pl.multiple_of((head_ref[8] ^ half) * (width // 2), HD) + low, size)
        mixed = acc_ref[:, lanes]
        for a_ref, w_ref, rows in zip((a0, a1), ((w0_mine, w0_other)[half], (w1_mine, w1_other)[half]), row_sets):
            mixed = mixed + dot(a_ref[...], head_rows(head_ref, w_ref, rows, pl.ds(low, size)))
        hidden = in_ref[:, lanes].astype(F32) + gate_ref[0:1, lanes] * mixed
        high = hidden.astype(BF16)
        stream_ref[:, lanes] = high
        small = (hidden - high.astype(F32)).astype(BF16)
        parts = (
            sum_lanes(hidden),
            sum_lanes(hidden * hidden),
            dot_t(lifted_ref[:, lanes], high),
            dot_t(lifted_ref[0:channels, lanes], small),
        )
        if total is None:
            total, squares, share, rest = parts
        else:
            total, squares = total + parts[0], squares + parts[1]
            share, rest = share + parts[2], rest + parts[3]
    mean = jnp.sum(total, axis=1, keepdims=True) * (1.0 / width)
    spread = jnp.sum(squares, axis=1, keepdims=True) - mean * mean * width
    stats = jnp.transpose(place((mean, spread), (row_count, HD)))
    mean_row, spread_row = stats[0:1], stats[1:2]
    extra = extra_ref[...].astype(F32)
    lift_head = extra[:, 0:1] + extra[:, 1:2] + extra[:, 2:3]
    share = share[0:channels] + share[channels:] + rest - lift_head * mean_row
    rows = [x.astype(F32) for x in split3(mean_row) + split3(spread_row)]
    rows = jnp.concatenate(rows + [jnp.zeros((10, row_count), F32)], axis=0)
    message_ref[0:channels, 0:row_count] = share.astype(BF16)
    message_ref[channels:, 0:row_count] = rows.astype(BF16)
    message_ref[0:channels, row_count:] = extra_ref[...]
    message_ref[channels:, row_count:] = jnp.zeros((16, HD), BF16)


def finish_kernel(m0, m1, m2, m3, latent_ref, step_ref, velocity_ref, updated_ref):
    channels, row_count = velocity_ref.shape
    refs = (m0, m1, m2, m3)

    def tree(values):
        return (values[0] + values[1]) + (values[2] + values[3])

    shares = [ref[0:channels, 0:row_count].astype(F32) for ref in refs]
    stats = [ref[channels:, 0:row_count].astype(F32) for ref in refs]
    extras = [ref[0:channels, row_count:].astype(F32) for ref in refs]
    means = [x[0:1] + x[1:2] + x[2:3] for x in stats]
    spreads = [x[3:4] + x[4:5] + x[5:6] for x in stats]
    lifts = [x[:, 0:1] + x[:, 1:2] + x[:, 2:3] for x in extras]
    shifts = [x[:, 3:4] + x[:, 4:5] + x[:, 5:6] for x in extras]
    mean = tree(means) * (1.0 / N_TENSOR)
    offsets = [x - mean for x in means]
    variance = tree(spreads) * (1.0 / D) + tree([x * x for x in offsets]) * (1.0 / N_TENSOR)
    inv_std = lax.rsqrt(variance + 1e-06)
    total = tree([s + o * b for s, o, b in zip(shares, offsets, lifts)])
    velocity = total * inv_std + tree(shifts)
    velocity_ref[...] = velocity
    updated_ref[...] = (latent_ref[...] + step_ref[0, 0] * velocity).astype(BF16)


def local(
    queries,
    keys,
    values,
    stream_in,
    out_weight,
    time_weight,
    head_weight,
    latent,
    new_noise,
    levels,
    timesteps,
):
    row_count, width = stream_in.shape
    channels = latent.shape[1]
    frame_index = lax.axis_index("frame")
    frame_count = lax.axis_size("frame")
    tensor_index = lax.axis_index("tensor")
    barrier = lax.optimization_barrier

    def columns(mask, low=0, size=width):
        start = (tensor_index ^ mask) * width + low
        return lax.dynamic_slice(out_weight, (0, start), (out_weight.shape[0], size))

    core_index = tensor_index % 2

    def heads_of(core):
        place_in_ring = (frame_index - core) % PART
        pair, member = place_in_ring // 2, place_in_ring % 2
        ahead, behind = (pair + 1) % SPREAD_HEADS, (pair + SPREAD_HEADS - 1) % SPREAD_HEADS
        return [
            pair,
            jnp.where(member == 1, ahead, behind),
            jnp.where(member == 1, behind, ahead),
            (pair + 2) % SPREAD_HEADS,
        ]

    half_index = frame_index // HALF_STRIDE % 2
    heads = jnp.stack(heads_of(core_index) + heads_of(1 - core_index) + [half_index]).astype(jnp.int32)
    kv_width, packed_width = 4 * HD, 5 * HD
    x1, x2, x3, own_kv, own_q = pl.pallas_call(
        pack_kernel,
        in_specs=[pl.BlockSpec(memory_space=pltpu.SMEM)] + [pl.BlockSpec(memory_space=pl.ANY)] * 3,
        out_specs=[pl.BlockSpec(memory_space=pl.ANY)] * 5,
        scratch_shapes=[pltpu.SemaphoreType.DMA((21,))],
        out_shape=[jax.ShapeDtypeStruct((row_count, packed_width), BF16)] * 3
        + [jax.ShapeDtypeStruct((row_count, kv_width), BF16), jax.ShapeDtypeStruct((row_count, 2 * HD), BF16)],
        compiler_params=params(),
        cost_estimate=SMALL,
    )(heads, queries, keys, values)
    x3 = spread(x3, 3)
    x2 = spread(x2, 2)
    x1 = spread(x1, 1)
    half_width = width // 2
    across = [peer(columns(mask, half_index * half_width, half_width), mask) for mask in (2, 3)]
    x3, across = barrier((x3, across))
    across_other = [swap_half(w) for w in across]
    partner = [swap_pair(own_kv)] + [swap_pair(x[:, :kv_width]) for x in (x1, x2, x3)]
    queries_in = (x1, x2, x3, own_q, own_q)
    query_lanes = ((kv_width, False),) * 3 + ((0, False), (HD, True))
    state = attend(
        queries_in, query_lanes, (own_kv, x1, x2, x3, *partner[:2]), None, 0, False, False
    )
    results = attend(queries_in[:3], query_lanes[:3], partner[2:], state, 0, True, False)
    mine = attend(queries_in[3:], query_lanes[3:], partner[2:], state, 3, True, True)
    results, across_other[0] = barrier((results, across_other[0]))
    back = [spread(x, i + 1, True) for i, x in enumerate(results)]
    back = jnp.concatenate(back, axis=1)

    weights = [columns(0), peer(columns(1), 1)]
    far_weights = [across[0], across_other[0], across[1], across_other[1]]

    t_now = lookup(timesteps, levels)
    t_next = lookup(timesteps, levels - 1)
    embedding = sinusoid(t_now, TFREQ).astype(BF16)
    step = ((t_next - t_now) / 1000.0).reshape(1, 1)
    head = head_weight.T
    gate, lifted, extra = pl.pallas_call(
        modulate_kernel,
        out_shape=[
            jax.ShapeDtypeStruct((8, width), F32),
            jax.ShapeDtypeStruct((2 * channels, width), BF16),
            jax.ShapeDtypeStruct((channels, HD), BF16),
        ],
        compiler_params=params(),
        cost_estimate=SMALL,
    )(embedding, time_weight, head)

    mine_all = [mine] + [peer(mine, mask) for mask in (1, 2, 3)]
    back_beside, back_across = peer(back, 1), peer(back, 2)
    back_last = peer(back_across, 1)
    mine_rows, back_rows = ((0, None), (4, None)), ((1, 2, 3), (5, 6, 7))
    acc = project(heads, mine_all[:2], weights, mine_rows)
    acc = project(heads, mine_all[2:], far_weights, mine_rows, acc)
    acc = project(heads, [back, back_beside], weights, back_rows, acc)

    def finish_hidden(*refs):
        hidden_kernel(back_rows, *refs)

    stream, message = pl.pallas_call(
        finish_hidden,
        in_specs=[pl.BlockSpec(memory_space=pltpu.SMEM)] + [pl.BlockSpec(memory_space=pltpu.VMEM)] * 11,
        out_shape=[
            jax.ShapeDtypeStruct((row_count, width), BF16),
            jax.ShapeDtypeStruct((channels + 16, row_count + HD), BF16),
        ],
        compiler_params=params(),
        cost_estimate=SMALL,
    )(heads, back_across, back_last, *far_weights, acc, stream_in, gate, lifted, extra)
    messages = [message] + [peer(message, mask) for mask in (1, 2, 3)]
    velocity, updated = pl.pallas_call(
        finish_kernel,
        in_specs=[pl.BlockSpec(memory_space=pltpu.VMEM)] * 5 + [pl.BlockSpec(memory_space=pltpu.SMEM)],
        out_shape=[
            jax.ShapeDtypeStruct((channels, row_count), F32),
            jax.ShapeDtypeStruct((channels, row_count), BF16),
        ],
        compiler_params=params(),
        cost_estimate=SMALL,
    )(*messages, latent.T, step)
    arrived = shifted(updated, "frame", -1).astype(F32)
    queue_next = jnp.where(frame_index == frame_count - 1, new_noise.T, arrived)
    return (stream, velocity.T, queue_next.T)


def solution(mesh):
    return jax.shard_map(
        local,
        mesh=mesh,
        in_specs=(
            P("frame", "tensor"),
            P("frame", "tensor"),
            P("frame", "tensor"),
            P("frame", "tensor"),
            P("tensor", None),
            P(None, None, "tensor"),
            P("tensor", None),
            P("frame", None),
            P(),
            P("frame"),
            P(),
        ),
        out_specs=(P("frame", "tensor"), P("frame", None), P("frame", None)),
        check_vma=False,
    )
```

```python
import math

import jax
import jax.numpy as jnp
from jax import lax
from jax.experimental import pallas as pl
from jax.experimental.pallas import tpu as pltpu
from jax.sharding import PartitionSpec as P

D = 5120
HD = 128
TFREQ = 256
PART = 8
N_TENSOR = 4
F32 = jnp.float32
BF16 = jnp.bfloat16
COLUMN_BLOCK = 256
SPREAD_HEADS = 4
SMALL = pl.CostEstimate(flops=1000, bytes_accessed=1000, transcendentals=0)
ATTEND_COST = pl.CostEstimate(flops=9_000_000_000, bytes_accessed=1000, transcendentals=0)
EXP_SCALE = HD ** (-0.5) / math.log(2.0)
VMEM_LIMIT = 16 * 1024 * 1024
COPY_LIMIT = 56 * 1024 * 1024


def params(limit=VMEM_LIMIT):
    return pltpu.CompilerParams(vmem_limit_bytes=limit)


def spread(x, distance, backward=False):
    pairs = []
    for frame in range(lax.axis_size("frame")):
        for core in range(N_TENSOR):
            at = (frame - core) % PART
            step = distance if (at + distance) % 2 == 0 else -distance
            target = frame // PART * PART + (frame + step) % PART
            pairs.append((frame * N_TENSOR + core, target * N_TENSOR + core))
    if backward:
        pairs = [(b, a) for a, b in pairs]
    return lax.ppermute(x, ("frame", "tensor"), pairs)


def swap_pair(x):
    pairs = []
    for frame in range(lax.axis_size("frame")):
        for core in range(N_TENSOR):
            at = (frame - core) % PART
            target = frame // PART * PART + ((at ^ 1) + core) % PART
            pairs.append((frame * N_TENSOR + core, target * N_TENSOR + core))
    return lax.ppermute(x, ("frame", "tensor"), pairs)


def across_both(x):
    pairs = []
    for frame in range(lax.axis_size("frame")):
        for at in range(N_TENSOR):
            pairs.append((frame * N_TENSOR + at, (frame ^ PART) * N_TENSOR + (at ^ 2)))
    return lax.ppermute(x, ("frame", "tensor"), pairs)


def peer(x, mask):
    return lax.ppermute(x, "tensor", [(i, i ^ mask) for i in range(N_TENSOR)])


def shifted(x, axis, by):
    length = lax.axis_size(axis)
    pairs = [(i, i + by) for i in range(length) if 0 <= i + by < length]
    return lax.ppermute(x, axis, pairs)


def sinusoid(time_values, freq_width):
    half_width = freq_width // 2
    frequencies = jnp.exp(
        -math.log(10000.0) * jnp.arange(half_width, dtype=jnp.float32) / half_width
    )
    angles = time_values[:, None] * frequencies[None, :]
    return jnp.concatenate([jnp.cos(angles), jnp.sin(angles)], axis=-1)


def lookup(table_values, positions):
    matches = jnp.arange(table_values.shape[0], dtype=jnp.int32)[None, :] == positions[:, None]
    return jnp.sum(jnp.where(matches, table_values[None, :], 0), axis=1).astype(jnp.float32)


def dot(a, b):
    return jnp.dot(a, b, preferred_element_type=F32)


def dot_t(a, b):
    return lax.dot_general(a, b, (((1,), (1,)), ((), ())), preferred_element_type=F32)


def split3(x):
    hi = x.astype(BF16)
    rest = x - hi.astype(F32)
    mid = rest.astype(BF16)
    return hi, mid, (rest - mid.astype(F32)).astype(BF16)


def pack_kernel(
    head_ref, q_hbm, k_hbm, v_hbm, x1_ref, x2_ref, x3_ref, kv_ref, q_out_ref, q_ref, k_ref, v_ref, sem
):
    common = pl.ds(SPREAD_HEADS * HD, HD)
    copies = [
        pltpu.make_async_copy(source, target, sem.at[at])
        for at, (source, target) in enumerate(((k_hbm, k_ref), (v_hbm, v_ref), (q_hbm, q_ref)))
    ]
    for copy in copies:
        copy.start()

    def lanes(at):
        return pl.ds(pl.multiple_of(head_ref[at] * HD, HD), HD)

    targets = ((3, x3_ref), (2, x2_ref), (1, x1_ref), (0, kv_ref))
    for slot, (copy, source) in enumerate(zip(copies[:2], (k_ref, v_ref))):
        copy.wait()
        for at, ref in targets:
            ref[:, slot * HD : (slot + 1) * HD] = source[:, lanes(at)]
            ref[:, (slot + 2) * HD : (slot + 3) * HD] = source[:, common]
    copies[2].wait()
    for at, ref in targets[:3]:
        ref[:, 4 * HD :] = q_ref[:, lanes(at)]
    q_out_ref[:, 0:HD] = q_ref[:, lanes(0)]
    q_out_ref[:, HD:] = q_ref[:, common]


def attend_kernel(query_lanes, block_count, first, last, *refs):
    refs = list(refs)
    q_refs = [refs.pop(0) for _ in query_lanes]
    blocks = [refs.pop(0) for _ in range(block_count)]
    if not first:
        acc_in, peak_in, total_in = refs.pop(0), refs.pop(0), refs.pop(0)
    row_count = q_refs[0].shape[0]
    for at, (q_ref, (q_low, shared)) in enumerate(zip(q_refs, query_lanes)):
        key_low = 2 * HD if shared else 0
        query = q_ref[:, q_low : q_low + HD]
        scores = [dot_t(query, ref[:, key_low : key_low + HD]) for ref in blocks]
        peak = max_of([jnp.max(s, axis=1, keepdims=True) for s in scores])
        rows = slice(at * row_count, (at + 1) * row_count)
        if not first:
            old_peak = peak_in[rows, 0:1]
            peak = jnp.maximum(peak, old_peak)
        acc = None
        total = None
        for s, ref in zip(scores, blocks):
            weights = jnp.exp2((s - peak) * EXP_SCALE)
            part = sum_lanes(weights)
            total = part if total is None else total + part
            mixed = dot(weights.astype(BF16), ref[:, key_low + HD : key_low + 2 * HD])
            acc = mixed if acc is None else acc + mixed
        if not first:
            shrink = jnp.exp2((old_peak - peak) * EXP_SCALE)
            acc = acc + acc_in[rows, :] * shrink
            total = total + total_in[rows, :] * shrink
        if last:
            out = (acc / jnp.sum(total, axis=1, keepdims=True)).astype(BF16)
            if at < PART // 2 - 1:
                refs[at][...] = out
            else:
                low = (at - PART // 2 + 1) * HD
                refs[-1][:, low : low + HD] = out
        else:
            refs[0][rows, :] = acc
            refs[1][rows, :] = jnp.broadcast_to(peak, acc.shape)
            refs[2][rows, :] = total


def max_of(values):
    result = values[0]
    for value in values[1:]:
        result = jnp.maximum(result, value)
    return result


def sum_lanes(x):
    result = x[:, :HD]
    for low in range(HD, x.shape[1], HD):
        result = result + x[:, low : low + HD]
    return result


def attend(queries, query_lanes, blocks, state, cost):
    row_count = queries[0].shape[0]
    operands = list(queries) + list(blocks)
    first = state is None
    if first:
        out_shape = [jax.ShapeDtypeStruct((row_count * len(queries), HD), F32)] * 3
    else:
        operands += list(state)
        out_shape = [jax.ShapeDtypeStruct((row_count, HD), BF16)] * 3
        out_shape += [jax.ShapeDtypeStruct((row_count, 2 * HD), BF16)]

    def body(*refs):
        attend_kernel(query_lanes, len(blocks), first, not first, *refs)

    return pl.pallas_call(body, out_shape=out_shape, compiler_params=params(), cost_estimate=cost)(*operands)


def modulate_kernel(embedding_ref, time_ref, head_ref, gate_ref, lifted_ref, extra_ref):
    width = gate_ref.shape[1]
    channels = head_ref.shape[0]
    embedding = jnp.broadcast_to(embedding_ref[...], (16, TFREQ))
    gate_ref[...] = dot(embedding, time_ref[0])[:8]
    shift = dot(embedding, time_ref[1])[:1]
    lift = 1.0 + dot(embedding, time_ref[2])[:1]
    head = head_ref[...].astype(F32)
    lifted = head * lift
    high = lifted.astype(BF16)
    low = (lifted - high.astype(F32)).astype(BF16)
    lifted_ref[0:channels] = high
    lifted_ref[channels:] = low
    lift_head = jnp.sum(high.astype(F32) + low.astype(F32), axis=1, keepdims=True)
    shift_head = jnp.sum(head * shift, axis=1, keepdims=True)
    extra_ref[...] = place(split3(lift_head) + split3(shift_head), extra_ref.shape).astype(BF16)


def place(pieces, shape):
    lane = lax.broadcasted_iota(jnp.int32, shape, 1)
    result = jnp.zeros(shape, F32)
    for at, piece in enumerate(pieces):
        result = jnp.where(lane == at, piece.astype(F32), result)
    return result


def head_rows(head_ref, w_ref, rows, lanes):
    parts = []
    for row in rows:
        if row is None:
            parts.append(w_ref[SPREAD_HEADS * HD : (SPREAD_HEADS + 1) * HD, lanes])
        else:
            parts.append(w_ref[pl.ds(pl.multiple_of(head_ref[row] * HD, HD), HD), lanes])
    return jnp.concatenate(parts, axis=0)


def mix_kernel(out_dtype, terms, with_base, head_ref, *refs):
    refs = list(refs)
    sources = []
    for input_count, weight_count, rows, column in terms:
        inputs = [refs.pop(0) for _ in range(input_count)]
        sources.append((inputs, [refs.pop(0) for _ in range(weight_count)], rows, column))
    base_ref = refs.pop(0) if with_base else None
    out_ref = refs[0]
    width = out_ref.shape[1]
    for low in range(0, width, COLUMN_BLOCK):
        lanes = pl.ds(low, COLUMN_BLOCK)
        acc = base_ref[:, lanes] if with_base else None
        for inputs, weights, rows, column in sources:
            offset = 0 if column is None else pl.multiple_of(head_ref[column] * width, HD)
            weight = head_rows(head_ref, weights[0], rows, pl.ds(offset + low, COLUMN_BLOCK))
            value = inputs[0][...]
            if len(inputs) > 1:
                value = jnp.concatenate([ref[...] for ref in inputs], axis=1)
            part = dot(value, weight)
            acc = part if acc is None else acc + part
        out_ref[:, lanes] = acc.astype(out_dtype)


def mix(heads, width, terms, out_dtype, base=None):
    shapes, operands = [], [heads]
    for inputs, weights, rows, column in terms:
        shapes.append((len(inputs), len(weights), rows, column))
        operands += [*inputs, *weights]
    if base is not None:
        operands.append(base)
    row_count = operands[1].shape[0]

    def body(*refs):
        mix_kernel(out_dtype, shapes, base is not None, *refs)

    return pl.pallas_call(
        body,
        in_specs=[pl.BlockSpec(memory_space=pltpu.SMEM)]
        + [pl.BlockSpec(memory_space=pltpu.VMEM)] * (len(operands) - 1),
        out_shape=jax.ShapeDtypeStruct((row_count, width), out_dtype),
        compiler_params=params(),
        cost_estimate=SMALL,
    )(*operands)


def hidden_kernel(
    acc_ref, other_ref, in_ref, gate_ref, lifted_ref, extra_ref, stream_ref, message_ref
):
    row_count, width = stream_ref.shape
    channels = extra_ref.shape[0]
    total = None
    squares = None
    share = None
    rest = None
    for low in range(0, width, COLUMN_BLOCK):
        lanes = slice(low, low + COLUMN_BLOCK)
        mixed = acc_ref[:, lanes] + other_ref[:, lanes].astype(F32)
        hidden = in_ref[:, lanes].astype(F32) + gate_ref[0:1, lanes] * mixed
        high = hidden.astype(BF16)
        stream_ref[:, lanes] = high
        small = (hidden - high.astype(F32)).astype(BF16)
        parts = (
            sum_lanes(hidden),
            sum_lanes(hidden * hidden),
            dot_t(lifted_ref[:, lanes], high),
            dot_t(lifted_ref[0:channels, lanes], small),
        )
        if total is None:
            total, squares, share, rest = parts
        else:
            total, squares = total + parts[0], squares + parts[1]
            share, rest = share + parts[2], rest + parts[3]
    mean = jnp.sum(total, axis=1, keepdims=True) * (1.0 / width)
    spread = jnp.sum(squares, axis=1, keepdims=True) - mean * mean * width
    stats = jnp.transpose(place((mean, spread), (row_count, HD)))
    mean_row, spread_row = stats[0:1], stats[1:2]
    extra = extra_ref[...].astype(F32)
    lift_head = extra[:, 0:1] + extra[:, 1:2] + extra[:, 2:3]
    share = share[0:channels] + share[channels:] + rest - lift_head * mean_row
    rows = [x.astype(F32) for x in split3(mean_row) + split3(spread_row)]
    rows = jnp.concatenate(rows + [jnp.zeros((10, row_count), F32)], axis=0)
    message_ref[0:channels, 0:row_count] = share.astype(BF16)
    message_ref[channels:, 0:row_count] = rows.astype(BF16)
    message_ref[0:channels, row_count:] = extra_ref[...]
    message_ref[channels:, row_count:] = jnp.zeros((16, HD), BF16)


def finish_kernel(m0, m1, m2, m3, latent_ref, step_ref, velocity_ref, updated_ref):
    channels, row_count = velocity_ref.shape
    refs = (m0, m1, m2, m3)

    def tree(values):
        return (values[0] + values[1]) + (values[2] + values[3])

    shares = [ref[0:channels, 0:row_count].astype(F32) for ref in refs]
    stats = [ref[channels:, 0:row_count].astype(F32) for ref in refs]
    extras = [ref[0:channels, row_count:].astype(F32) for ref in refs]
    means = [x[0:1] + x[1:2] + x[2:3] for x in stats]
    spreads = [x[3:4] + x[4:5] + x[5:6] for x in stats]
    lifts = [x[:, 0:1] + x[:, 1:2] + x[:, 2:3] for x in extras]
    shifts = [x[:, 3:4] + x[:, 4:5] + x[:, 5:6] for x in extras]
    mean = tree(means) * (1.0 / N_TENSOR)
    offsets = [x - mean for x in means]
    variance = tree(spreads) * (1.0 / D) + tree([x * x for x in offsets]) * (1.0 / N_TENSOR)
    inv_std = lax.rsqrt(variance + 1e-06)
    total = tree([s + o * b for s, o, b in zip(shares, offsets, lifts)])
    velocity = total * inv_std + tree(shifts)
    velocity_ref[...] = velocity
    updated_ref[...] = (latent_ref[...] + step_ref[0, 0] * velocity).astype(BF16)


def local(
    queries,
    keys,
    values,
    stream_in,
    out_weight,
    time_weight,
    head_weight,
    latent,
    new_noise,
    levels,
    timesteps,
):
    row_count, width = stream_in.shape
    channels = latent.shape[1]
    frame_index = lax.axis_index("frame")
    frame_count = lax.axis_size("frame")
    tensor_index = lax.axis_index("tensor")
    barrier = lax.optimization_barrier

    t_now = lookup(timesteps, levels)
    t_next = lookup(timesteps, levels - 1)
    embedding = sinusoid(t_now, TFREQ).astype(BF16)
    step = ((t_next - t_now) / 1000.0).reshape(1, 1)
    head = head_weight.T
    gate, lifted, extra = pl.pallas_call(
        modulate_kernel,
        out_shape=[
            jax.ShapeDtypeStruct((8, width), F32),
            jax.ShapeDtypeStruct((2 * channels, width), BF16),
            jax.ShapeDtypeStruct((channels, HD), BF16),
        ],
        compiler_params=params(),
        cost_estimate=SMALL,
    )(embedding, time_weight, head)
    tables = (gate, lifted, extra, step)

    core_index, side = tensor_index % 2, tensor_index // 2
    at = (frame_index - core_index) % PART
    pair, member = at // 2, at % 2
    ahead, behind = (pair + 1) % SPREAD_HEADS, (pair + SPREAD_HEADS - 1) % SPREAD_HEADS
    heads = jnp.stack(
        [
            pair,
            jnp.where(member == 1, ahead, behind),
            jnp.where(member == 1, behind, ahead),
            (pair + 2) % SPREAD_HEADS,
            side,
            core_index,
            1 - core_index,
        ]
    ).astype(jnp.int32)
    depth = out_weight.shape[0]
    kv_width, packed_width = 4 * HD, 5 * HD
    in_smem = pl.BlockSpec(memory_space=pltpu.SMEM)
    in_hbm = pl.BlockSpec(memory_space=pltpu.HBM)
    x1, x2, x3, own_kv, own_q = pl.pallas_call(
        pack_kernel,
        in_specs=[in_smem] + [in_hbm] * 3,
        out_specs=[pl.BlockSpec(memory_space=pltpu.VMEM)] * 5,
        scratch_shapes=[pltpu.VMEM(queries.shape, BF16)] * 3 + [pltpu.SemaphoreType.DMA((3,))],
        out_shape=[jax.ShapeDtypeStruct((row_count, packed_width), BF16)] * 3
        + [jax.ShapeDtypeStruct((row_count, kv_width), BF16), jax.ShapeDtypeStruct((row_count, 2 * HD), BF16)],
        compiler_params=params(COPY_LIMIT),
        cost_estimate=SMALL,
    )(heads, queries, keys, values)

    x3 = spread(x3, 3)
    x2 = spread(x2, 2)
    x1 = spread(x1, 1)
    partner = [swap_pair(own_kv)]
    far = [
        lax.dynamic_slice(out_weight, (0, ((1 - side) * 2 + core) * width), (depth, width))
        for core in (core_index, 1 - core_index)
    ]
    far = [peer(far[0], 2), across_both(far[1])]
    own_weight = lax.dynamic_slice(out_weight, (0, side * 2 * width), (depth, 2 * width))
    x1, x2, x3, partner, own_weight, tables = barrier((x1, x2, x3, partner, own_weight, tables))
    gate, lifted, extra, step = tables
    partner += [swap_pair(x[:, :kv_width]) for x in (x1, x2, x3)]
    queries_in = (x1, x2, x3, own_q, own_q)
    query_lanes = ((kv_width, False),) * 3 + ((0, False), (HD, True))
    state = attend(queries_in, query_lanes, (own_kv, x1, x2, x3, partner[0]), None, ATTEND_COST)
    state, far = barrier((state, far))
    *results, mine = attend(queries_in, query_lanes, partner[1:], state, SMALL)
    back = [spread(x, i + 1, True) for i, x in enumerate(results)]
    back_across = [peer(x, 2) for x in back]
    mine_across = peer(mine, 2)
    mine_rows, back_rows = (0, None), (1, 2, 3)
    sums = [
        mix(
            heads,
            width,
            [
                ([mine], [own_weight], mine_rows, column),
                (back, [own_weight], back_rows, column),
                ([mine_across], [weight], mine_rows, None),
            ],
            F32,
        )
        for column, weight in ((6, far[1]), (5, far[0]))
    ]
    sent = mix(heads, width, [(back_across, [far[1]], back_rows, None)], BF16, sums[0])
    kept = mix(heads, width, [(back_across, [far[0]], back_rows, None)], F32, sums[1])
    received = peer(sent, 1)

    stream, message = pl.pallas_call(
        hidden_kernel,
        out_shape=[
            jax.ShapeDtypeStruct((row_count, width), BF16),
            jax.ShapeDtypeStruct((channels + 16, row_count + HD), BF16),
        ],
        compiler_params=params(),
        cost_estimate=SMALL,
    )(kept, received, stream_in, gate, lifted, extra)
    messages = [message] + [peer(message, mask) for mask in (1, 2, 3)]
    velocity, updated = pl.pallas_call(
        finish_kernel,
        in_specs=[pl.BlockSpec(memory_space=pltpu.VMEM)] * 5 + [pl.BlockSpec(memory_space=pltpu.SMEM)],
        out_shape=[
            jax.ShapeDtypeStruct((channels, row_count), F32),
            jax.ShapeDtypeStruct((channels, row_count), BF16),
        ],
        compiler_params=params(),
        cost_estimate=SMALL,
    )(*messages, latent.T, step)
    arrived = shifted(updated, "frame", -1).astype(F32)
    queue_next = jnp.where(frame_index == frame_count - 1, new_noise.T, arrived)
    return (stream, velocity.T, queue_next.T)


def solution(mesh):
    return jax.shard_map(
        local,
        mesh=mesh,
        in_specs=(
            P("frame", "tensor"),
            P("frame", "tensor"),
            P("frame", "tensor"),
            P("frame", "tensor"),
            P("tensor", None),
            P(None, None, "tensor"),
            P("tensor", None),
            P("frame", None),
            P(),
            P("frame"),
            P(),
        ),
        out_specs=(P("frame", "tensor"), P("frame", None), P("frame", None)),
        check_vma=False,
    )
```

```python
import math

import jax
import jax.numpy as jnp
from jax import lax
from jax.experimental import pallas as pl
from jax.experimental.pallas import tpu as pltpu
from jax.sharding import PartitionSpec as P

D = 5120
HD = 128
TFREQ = 256
PART = 8
N_TENSOR = 4
F32 = jnp.float32
BF16 = jnp.bfloat16
COLUMN_BLOCK = 256
SPREAD_HEADS = 4
STAT_ROWS = 32
SMALL = pl.CostEstimate(flops=1000, bytes_accessed=1000, transcendentals=0)
ATTEND_COST = pl.CostEstimate(flops=9_000_000_000, bytes_accessed=1000, transcendentals=0)
EXP_SCALE = HD ** (-0.5) / math.log(2.0)
VMEM_LIMIT = 16 * 1024 * 1024
COPY_LIMIT = 56 * 1024 * 1024


def params(limit=VMEM_LIMIT):
    return pltpu.CompilerParams(vmem_limit_bytes=limit)


def spread(x, distance, backward=False):
    pairs = []
    for frame in range(lax.axis_size("frame")):
        for core in range(N_TENSOR):
            at = (frame - core) % PART
            step = distance if (at + distance) % 2 == 0 else -distance
            target = frame // PART * PART + (frame + step) % PART
            pairs.append((frame * N_TENSOR + core, target * N_TENSOR + core))
    if backward:
        pairs = [(b, a) for a, b in pairs]
    return lax.ppermute(x, ("frame", "tensor"), pairs)


def swap_pair(x):
    pairs = []
    for frame in range(lax.axis_size("frame")):
        for core in range(N_TENSOR):
            at = (frame - core) % PART
            target = frame // PART * PART + ((at ^ 1) + core) % PART
            pairs.append((frame * N_TENSOR + core, target * N_TENSOR + core))
    return lax.ppermute(x, ("frame", "tensor"), pairs)


def across_both(x):
    pairs = []
    for frame in range(lax.axis_size("frame")):
        for at in range(N_TENSOR):
            pairs.append((frame * N_TENSOR + at, (frame ^ PART) * N_TENSOR + (at ^ 2)))
    return lax.ppermute(x, ("frame", "tensor"), pairs)


def peer(x, mask):
    return lax.ppermute(x, "tensor", [(i, i ^ mask) for i in range(N_TENSOR)])


def shifted(x, axis, by):
    length = lax.axis_size(axis)
    pairs = [(i, i + by) for i in range(length) if 0 <= i + by < length]
    return lax.ppermute(x, axis, pairs)


def sinusoid(time_values, freq_width):
    half_width = freq_width // 2
    frequencies = jnp.exp(
        -math.log(10000.0) * jnp.arange(half_width, dtype=jnp.float32) / half_width
    )
    angles = time_values[:, None] * frequencies[None, :]
    return jnp.concatenate([jnp.cos(angles), jnp.sin(angles)], axis=-1)


def lookup(table_values, positions):
    matches = jnp.arange(table_values.shape[0], dtype=jnp.int32)[None, :] == positions[:, None]
    return jnp.sum(jnp.where(matches, table_values[None, :], 0), axis=1).astype(jnp.float32)


def dot(a, b):
    return jnp.dot(a, b, preferred_element_type=F32)


def dot_t(a, b):
    return lax.dot_general(a, b, (((1,), (1,)), ((), ())), preferred_element_type=F32)


def split3(x):
    hi = x.astype(BF16)
    rest = x - hi.astype(F32)
    mid = rest.astype(BF16)
    return hi, mid, (rest - mid.astype(F32)).astype(BF16)


def pack_kernel(
    head_ref, q_hbm, k_hbm, v_hbm, x1_ref, x2_ref, x3_ref, kv_ref, q_out_ref, q_ref, k_ref, v_ref, sem
):
    common = pl.ds(SPREAD_HEADS * HD, HD)
    copies = [
        pltpu.make_async_copy(source, target, sem.at[at])
        for at, (source, target) in enumerate(((k_hbm, k_ref), (v_hbm, v_ref), (q_hbm, q_ref)))
    ]
    for copy in copies:
        copy.start()

    def lanes(at):
        return pl.ds(pl.multiple_of(head_ref[at] * HD, HD), HD)

    targets = ((3, x3_ref), (2, x2_ref), (1, x1_ref), (0, kv_ref))
    for slot, (copy, source) in enumerate(zip(copies[:2], (k_ref, v_ref))):
        copy.wait()
        for at, ref in targets:
            ref[:, slot * HD : (slot + 1) * HD] = source[:, lanes(at)]
        kv_ref[:, (slot + 2) * HD : (slot + 3) * HD] = source[:, common]
    copies[2].wait()
    for at, ref in targets[:3]:
        ref[:, 2 * HD : 3 * HD] = q_ref[:, lanes(at)]
        ref[:, 3 * HD :] = q_ref[:, common]
    q_out_ref[:, 0:HD] = q_ref[:, lanes(0)]
    q_out_ref[:, HD:] = q_ref[:, common]


def softmax_block(query, keys, values, old=None):
    scores = [dot_t(query, key) for key in keys]
    peak = max_of([jnp.max(s, axis=1, keepdims=True) for s in scores])
    if old is not None:
        old_acc, old_peak, old_total = old
        peak = jnp.maximum(peak, old_peak)
    acc = None
    total = None
    for s, value in zip(scores, values):
        weights = jnp.exp2((s - peak) * EXP_SCALE)
        part = sum_lanes(weights)
        total = part if total is None else total + part
        mixed = dot(weights.astype(BF16), value)
        acc = mixed if acc is None else acc + mixed
    if old is not None:
        shrink = jnp.exp2((old_peak - peak) * EXP_SCALE)
        acc = acc + old_acc * shrink
        total = total + old_total * shrink
    return acc, peak, total


def attend_kernel(operand_count, last, *refs):
    refs = list(refs)
    far_q_ref, own_q_ref = refs.pop(0), refs.pop(0)
    row_count = own_q_ref.shape[0]
    far_count = far_q_ref.shape[0] // row_count
    queries = [far_q_ref[at * row_count : (at + 1) * row_count, 0:HD] for at in range(far_count)]
    queries.append(own_q_ref[:, 0:HD])
    blocks = []
    for _ in range(operand_count):
        ref = refs.pop(0)
        blocks += [(ref, low) for low in range(0, ref.shape[0], row_count)]
    states = [refs.pop(0) for _ in range(3)] if last else None
    keys = [ref[low : low + row_count, 0:HD] for ref, low in blocks]
    values = [ref[low : low + row_count, HD : 2 * HD] for ref, low in blocks]
    for at, query in enumerate(queries):
        rows = slice(at * row_count, (at + 1) * row_count)
        old = (states[0][rows, :], states[1][rows, 0:1], states[2][rows, :]) if last else None
        acc, peak, total = softmax_block(query, keys, values, old)
        if last:
            refs[at][...] = (acc / jnp.sum(total, axis=1, keepdims=True)).astype(BF16)
        else:
            refs[0][rows, :] = acc
            refs[1][rows, :] = jnp.broadcast_to(peak, acc.shape)
            refs[2][rows, :] = total


def gather_kernel(x1_ref, x2_ref, x3_ref, kv_ref, q_ref):
    row_count = x1_ref.shape[0]
    for at, ref in enumerate((x1_ref, x2_ref, x3_ref)):
        rows = slice(at * row_count, (at + 1) * row_count)
        kv_ref[rows, :] = ref[:, 0 : 2 * HD]
        q_ref[rows, :] = ref[:, 2 * HD :]


def common_kernel(own_q_ref, far_q_ref, kv0, kv1, *refs):
    row_count = own_q_ref.shape[0]
    keys = [ref[:, 2 * HD : 3 * HD] for ref in (kv0, kv1)]
    values = [ref[:, 3 * HD :] for ref in (kv0, kv1)]
    queries = [far_q_ref[at * row_count : (at + 1) * row_count, HD:] for at in range(3)]
    for at, query in enumerate((*queries, own_q_ref[:, HD:])):
        acc, peak, total = softmax_block(query, keys, values)
        total = jnp.sum(total, axis=1, keepdims=True)
        if at == 3:
            refs[3][...] = acc
            refs[4][...] = jnp.broadcast_to(peak, acc.shape)
            refs[5][...] = jnp.broadcast_to(total, acc.shape)
            continue
        refs[at][0:row_count, :] = (acc / total).astype(BF16)
        rows = []
        for value in (peak, total):
            for low in range(0, row_count, HD):
                block = jnp.broadcast_to(value[low : low + HD], (HD, HD))
                rows += [x.astype(F32) for x in split3(jnp.transpose(block)[0:1])]
        rows += [jnp.zeros((STAT_ROWS - len(rows), HD), F32)]
        refs[at][row_count:, :] = jnp.concatenate(rows, axis=0).astype(BF16)


def merge_kernel(m1, m2, m3, acc_ref, peak_ref, total_ref, own_ref, out_ref):
    out_ref[:, 0:HD] = own_ref[...]
    row_count = acc_ref.shape[0]
    stats = [ref[row_count:, :].astype(F32) for ref in (m1, m2, m3)]

    def column(stat, at):
        row = stat[3 * at : 3 * at + 1] + stat[3 * at + 1 : 3 * at + 2] + stat[3 * at + 2 : 3 * at + 3]
        return jnp.transpose(jnp.broadcast_to(row, (HD, HD)))

    count = row_count // HD
    for at in range(count):
        rows = slice(at * HD, (at + 1) * HD)
        peaks = [peak_ref[rows, :]] + [column(stat, at) for stat in stats]
        totals = [total_ref[rows, :]] + [column(stat, count + at) for stat in stats]
        top = max_of(peaks)
        shares = [jnp.exp2((peak - top) * EXP_SCALE) for peak in peaks]
        numerator = acc_ref[rows, :] * shares[0]
        denominator = totals[0] * shares[0]
        for ref, share, total in zip((m1, m2, m3), shares[1:], totals[1:]):
            weight = share * total
            numerator = numerator + ref[rows, :].astype(F32) * weight
            denominator = denominator + weight
        out_ref[rows, HD:] = (numerator / denominator).astype(BF16)


def max_of(values):
    result = values[0]
    for value in values[1:]:
        result = jnp.maximum(result, value)
    return result


def sum_lanes(x):
    result = x[:, :HD]
    for low in range(HD, x.shape[1], HD):
        result = result + x[:, low : low + HD]
    return result


def attend(far_queries, own_queries, blocks, state, cost):
    row_count = own_queries.shape[0]
    query_rows = row_count + far_queries.shape[0]
    operands = [far_queries, own_queries, *blocks] + ([] if state is None else list(state))
    if state is not None:
        out_shape = [jax.ShapeDtypeStruct((row_count, HD), BF16)] * (query_rows // row_count)
    else:
        out_shape = [jax.ShapeDtypeStruct((query_rows, HD), F32)] * 3

    def body(*refs):
        attend_kernel(len(blocks), state is not None, *refs)

    return pl.pallas_call(body, out_shape=out_shape, compiler_params=params(), cost_estimate=cost)(*operands)


def modulate_kernel(embedding_ref, time_ref, head_ref, gate_ref, lifted_ref, extra_ref):
    width = gate_ref.shape[1]
    channels = head_ref.shape[0]
    embedding = jnp.broadcast_to(embedding_ref[...], (16, TFREQ))
    gate_ref[...] = dot(embedding, time_ref[0])[:8]
    shift = dot(embedding, time_ref[1])[:1]
    lift = 1.0 + dot(embedding, time_ref[2])[:1]
    head = head_ref[...].astype(F32)
    lifted = head * lift
    high = lifted.astype(BF16)
    low = (lifted - high.astype(F32)).astype(BF16)
    lifted_ref[0:channels] = high
    lifted_ref[channels:] = low
    lift_head = jnp.sum(high.astype(F32) + low.astype(F32), axis=1, keepdims=True)
    shift_head = jnp.sum(head * shift, axis=1, keepdims=True)
    extra_ref[...] = place(split3(lift_head) + split3(shift_head), extra_ref.shape).astype(BF16)


def place(pieces, shape):
    lane = lax.broadcasted_iota(jnp.int32, shape, 1)
    result = jnp.zeros(shape, F32)
    for at, piece in enumerate(pieces):
        result = jnp.where(lane == at, piece.astype(F32), result)
    return result


def head_rows(head_ref, w_ref, rows, lanes):
    parts = []
    for row in rows:
        if row is None:
            parts.append(w_ref[SPREAD_HEADS * HD : (SPREAD_HEADS + 1) * HD, lanes])
        else:
            parts.append(w_ref[pl.ds(pl.multiple_of(head_ref[row] * HD, HD), HD), lanes])
    return jnp.concatenate(parts, axis=0)


def mix_kernel(out_dtype, terms, with_base, head_ref, *refs):
    refs = list(refs)
    sources = []
    for input_count, weight_count, rows, column in terms:
        inputs = [refs.pop(0) for _ in range(input_count)]
        sources.append((inputs, [refs.pop(0) for _ in range(weight_count)], rows, column))
    base_ref = refs.pop(0) if with_base else None
    out_ref = refs[0]
    width = out_ref.shape[1]
    for low in range(0, width, COLUMN_BLOCK):
        lanes = pl.ds(low, COLUMN_BLOCK)
        acc = base_ref[:, lanes] if with_base else None
        for inputs, weights, rows, column in sources:
            offset = 0 if column is None else pl.multiple_of(head_ref[column] * width, HD)
            weight = head_rows(head_ref, weights[0], rows, pl.ds(offset + low, COLUMN_BLOCK))
            value = inputs[0][...]
            if len(inputs) > 1:
                value = jnp.concatenate([ref[...] for ref in inputs], axis=1)
            part = dot(value, weight)
            acc = part if acc is None else acc + part
        out_ref[:, lanes] = acc.astype(out_dtype)


def mix(heads, width, terms, out_dtype, base=None):
    shapes, operands = [], [heads]
    for inputs, weights, rows, column in terms:
        shapes.append((len(inputs), len(weights), rows, column))
        operands += [*inputs, *weights]
    if base is not None:
        operands.append(base)
    row_count = operands[1].shape[0]

    def body(*refs):
        mix_kernel(out_dtype, shapes, base is not None, *refs)

    return pl.pallas_call(
        body,
        in_specs=[pl.BlockSpec(memory_space=pltpu.SMEM)]
        + [pl.BlockSpec(memory_space=pltpu.VMEM)] * (len(operands) - 1),
        out_shape=jax.ShapeDtypeStruct((row_count, width), out_dtype),
        compiler_params=params(),
        cost_estimate=SMALL,
    )(*operands)


def hidden_kernel(
    acc_ref, other_ref, in_ref, gate_ref, lifted_ref, extra_ref, stream_ref, message_ref
):
    row_count, width = stream_ref.shape
    channels = extra_ref.shape[0]
    total = None
    squares = None
    share = None
    rest = None
    for low in range(0, width, COLUMN_BLOCK):
        lanes = slice(low, low + COLUMN_BLOCK)
        mixed = acc_ref[:, lanes] + other_ref[:, lanes].astype(F32)
        hidden = in_ref[:, lanes].astype(F32) + gate_ref[0:1, lanes] * mixed
        high = hidden.astype(BF16)
        stream_ref[:, lanes] = high
        small = (hidden - high.astype(F32)).astype(BF16)
        parts = (
            sum_lanes(hidden),
            sum_lanes(hidden * hidden),
            dot_t(lifted_ref[:, lanes], high),
            dot_t(lifted_ref[0:channels, lanes], small),
        )
        if total is None:
            total, squares, share, rest = parts
        else:
            total, squares = total + parts[0], squares + parts[1]
            share, rest = share + parts[2], rest + parts[3]
    mean = jnp.sum(total, axis=1, keepdims=True) * (1.0 / width)
    spread = jnp.sum(squares, axis=1, keepdims=True) - mean * mean * width
    stats = jnp.transpose(place((mean, spread), (row_count, HD)))
    mean_row, spread_row = stats[0:1], stats[1:2]
    extra = extra_ref[...].astype(F32)
    lift_head = extra[:, 0:1] + extra[:, 1:2] + extra[:, 2:3]
    share = share[0:channels] + share[channels:] + rest - lift_head * mean_row
    rows = [x.astype(F32) for x in split3(mean_row) + split3(spread_row)]
    rows = jnp.concatenate(rows + [jnp.zeros((10, row_count), F32)], axis=0)
    message_ref[0:channels, 0:row_count] = share.astype(BF16)
    message_ref[channels:, 0:row_count] = rows.astype(BF16)
    message_ref[0:channels, row_count:] = extra_ref[...]
    message_ref[channels:, row_count:] = jnp.zeros((16, HD), BF16)


def finish_kernel(m0, m1, m2, m3, latent_ref, step_ref, velocity_ref, updated_ref):
    channels, row_count = velocity_ref.shape
    refs = (m0, m1, m2, m3)

    def tree(values):
        return (values[0] + values[1]) + (values[2] + values[3])

    shares = [ref[0:channels, 0:row_count].astype(F32) for ref in refs]
    stats = [ref[channels:, 0:row_count].astype(F32) for ref in refs]
    extras = [ref[0:channels, row_count:].astype(F32) for ref in refs]
    means = [x[0:1] + x[1:2] + x[2:3] for x in stats]
    spreads = [x[3:4] + x[4:5] + x[5:6] for x in stats]
    lifts = [x[:, 0:1] + x[:, 1:2] + x[:, 2:3] for x in extras]
    shifts = [x[:, 3:4] + x[:, 4:5] + x[:, 5:6] for x in extras]
    mean = tree(means) * (1.0 / N_TENSOR)
    offsets = [x - mean for x in means]
    variance = tree(spreads) * (1.0 / D) + tree([x * x for x in offsets]) * (1.0 / N_TENSOR)
    inv_std = lax.rsqrt(variance + 1e-06)
    total = tree([s + o * b for s, o, b in zip(shares, offsets, lifts)])
    velocity = total * inv_std + tree(shifts)
    velocity_ref[...] = velocity
    updated_ref[...] = (latent_ref[...] + step_ref[0, 0] * velocity).astype(BF16)


def local(
    queries,
    keys,
    values,
    stream_in,
    out_weight,
    time_weight,
    head_weight,
    latent,
    new_noise,
    levels,
    timesteps,
):
    row_count, width = stream_in.shape
    channels = latent.shape[1]
    frame_index = lax.axis_index("frame")
    frame_count = lax.axis_size("frame")
    tensor_index = lax.axis_index("tensor")
    barrier = lax.optimization_barrier

    t_now = lookup(timesteps, levels)
    t_next = lookup(timesteps, levels - 1)
    embedding = sinusoid(t_now, TFREQ).astype(BF16)
    step = ((t_next - t_now) / 1000.0).reshape(1, 1)
    head = head_weight.T
    gate, lifted, extra = pl.pallas_call(
        modulate_kernel,
        out_shape=[
            jax.ShapeDtypeStruct((8, width), F32),
            jax.ShapeDtypeStruct((2 * channels, width), BF16),
            jax.ShapeDtypeStruct((channels, HD), BF16),
        ],
        compiler_params=params(),
        cost_estimate=SMALL,
    )(embedding, time_weight, head)
    tables = (gate, lifted, extra, step)

    core_index, side = tensor_index % 2, tensor_index // 2
    at = (frame_index - core_index) % PART
    pair, member = at // 2, at % 2
    ahead, behind = (pair + 1) % SPREAD_HEADS, (pair + SPREAD_HEADS - 1) % SPREAD_HEADS
    heads = jnp.stack(
        [
            pair,
            jnp.where(member == 1, ahead, behind),
            jnp.where(member == 1, behind, ahead),
            (pair + 2) % SPREAD_HEADS,
            side,
            core_index,
            1 - core_index,
        ]
    ).astype(jnp.int32)
    depth = out_weight.shape[0]
    kv_width, packed_width = 2 * HD, 4 * HD
    in_smem = pl.BlockSpec(memory_space=pltpu.SMEM)
    in_hbm = pl.BlockSpec(memory_space=pltpu.HBM)
    x1, x2, x3, own_kv, own_q = pl.pallas_call(
        pack_kernel,
        in_specs=[in_smem] + [in_hbm] * 3,
        out_specs=[pl.BlockSpec(memory_space=pltpu.VMEM)] * 5,
        scratch_shapes=[pltpu.VMEM(queries.shape, BF16)] * 3 + [pltpu.SemaphoreType.DMA((3,))],
        out_shape=[jax.ShapeDtypeStruct((row_count, packed_width), BF16)] * 3
        + [jax.ShapeDtypeStruct((row_count, packed_width), BF16), jax.ShapeDtypeStruct((row_count, 2 * HD), BF16)],
        compiler_params=params(COPY_LIMIT),
        cost_estimate=SMALL,
    )(heads, queries, keys, values)

    x3 = spread(x3, 3)
    x2 = spread(x2, 2)
    x1 = spread(x1, 1)
    partner = [swap_pair(own_kv)]
    partner[0], out_weight = barrier((partner[0], out_weight))
    far = [
        lax.dynamic_slice(out_weight, (0, ((1 - side) * 2 + core) * width), (depth, width))
        for core in (core_index, 1 - core_index)
    ]
    far = [peer(far[0], 2), across_both(far[1])]
    own_weight = lax.dynamic_slice(out_weight, (0, side * 2 * width), (depth, 2 * width))
    x1, x2, x3, partner, own_weight, tables = barrier((x1, x2, x3, partner, own_weight, tables))
    gate, lifted, extra, step = tables
    far_kv, far_q = pl.pallas_call(
        gather_kernel,
        out_shape=[jax.ShapeDtypeStruct((3 * row_count, kv_width), BF16)] * 2,
        compiler_params=params(),
        cost_estimate=SMALL,
    )(x1, x2, x3)
    swapped = swap_pair(far_kv)
    *parts, acc, peak, total = pl.pallas_call(
        common_kernel,
        out_shape=[jax.ShapeDtypeStruct((row_count + STAT_ROWS, HD), BF16)] * 3
        + [jax.ShapeDtypeStruct((row_count, HD), F32)] * 3,
        compiler_params=params(),
        cost_estimate=SMALL,
    )(own_q, far_q, own_kv, partner[0])
    state = attend(far_q, own_q, (own_kv, partner[0], far_kv), None, ATTEND_COST)
    parts[0], state = barrier((parts[0], state))
    parts = [spread(x, i + 1, True) for i, x in enumerate(parts)]
    *results, own_result = attend(far_q, own_q, (swapped,), state, SMALL)
    results, own_result, far = barrier((results, own_result, far))
    mine = pl.pallas_call(
        merge_kernel,
        out_shape=jax.ShapeDtypeStruct((row_count, 2 * HD), BF16),
        compiler_params=params(),
        cost_estimate=SMALL,
    )(*parts, acc, peak, total, own_result)
    back, back_across = [None] * 3, [None] * 3
    for at in (2, 1, 0):
        back[at] = spread(results[at], at + 1, True)
    for at in (0, 1, 2):
        back_across[at] = peer(back[at], 2)
    mine_across = peer(mine, 2)
    mine_rows, back_rows = (0, None), (1, 2, 3)
    sums = [
        mix(
            heads,
            width,
            [
                ([mine], [own_weight], mine_rows, column),
                (back, [own_weight], back_rows, column),
                ([mine_across], [weight], mine_rows, None),
            ],
            F32,
        )
        for column, weight in ((6, far[1]), (5, far[0]))
    ]
    sent = mix(heads, width, [(back_across, [far[1]], back_rows, None)], BF16, sums[0])
    kept = mix(heads, width, [(back_across, [far[0]], back_rows, None)], F32, sums[1])
    received = peer(sent, 1)

    stream, message = pl.pallas_call(
        hidden_kernel,
        out_shape=[
            jax.ShapeDtypeStruct((row_count, width), BF16),
            jax.ShapeDtypeStruct((channels + 16, row_count + HD), BF16),
        ],
        compiler_params=params(),
        cost_estimate=SMALL,
    )(kept, received, stream_in, gate, lifted, extra)
    messages = [message] + [peer(message, mask) for mask in (1, 2, 3)]
    velocity, updated = pl.pallas_call(
        finish_kernel,
        in_specs=[pl.BlockSpec(memory_space=pltpu.VMEM)] * 5 + [pl.BlockSpec(memory_space=pltpu.SMEM)],
        out_shape=[
            jax.ShapeDtypeStruct((channels, row_count), F32),
            jax.ShapeDtypeStruct((channels, row_count), BF16),
        ],
        compiler_params=params(),
        cost_estimate=SMALL,
    )(*messages, latent.T, step)
    arrived = shifted(updated, "frame", -1).astype(F32)
    queue_next = jnp.where(frame_index == frame_count - 1, new_noise.T, arrived)
    return (stream, velocity.T, queue_next.T)


def solution(mesh):
    return jax.shard_map(
        local,
        mesh=mesh,
        in_specs=(
            P("frame", "tensor"),
            P("frame", "tensor"),
            P("frame", "tensor"),
            P("frame", "tensor"),
            P("tensor", None),
            P(None, None, "tensor"),
            P("tensor", None),
            P("frame", None),
            P(),
            P("frame"),
            P(),
        ),
        out_specs=(P("frame", "tensor"), P("frame", None), P("frame", None)),
        check_vma=False,
    )
```

```python
import math

import jax
import jax.numpy as jnp
from jax import lax
from jax.experimental import pallas as pl
from jax.experimental.pallas import tpu as pltpu
from jax.sharding import PartitionSpec as P

D = 5120
HD = 128
TFREQ = 256
PART = 8
N_TENSOR = 4
F32 = jnp.float32
BF16 = jnp.bfloat16
COLUMN_BLOCK = 256
SPREAD_HEADS = 4
STAT_ROWS = 32
SMALL = pl.CostEstimate(flops=1000, bytes_accessed=1000, transcendentals=0)
ATTEND_COST = pl.CostEstimate(flops=9_000_000_000, bytes_accessed=1000, transcendentals=0)
EXP_SCALE = HD ** (-0.5) / math.log(2.0)
VMEM_LIMIT = 16 * 1024 * 1024
COPY_LIMIT = 56 * 1024 * 1024


def params(limit=VMEM_LIMIT):
    return pltpu.CompilerParams(vmem_limit_bytes=limit)


def spread(x, distance, backward=False):
    pairs = []
    for frame in range(lax.axis_size("frame")):
        for core in range(N_TENSOR):
            at = (frame - core) % PART
            step = distance if (at + distance) % 2 == 0 else -distance
            target = frame // PART * PART + (frame + step) % PART
            pairs.append((frame * N_TENSOR + core, target * N_TENSOR + core))
    if backward:
        pairs = [(b, a) for a, b in pairs]
    return lax.ppermute(x, ("frame", "tensor"), pairs)


def swap_pair(x):
    pairs = []
    for frame in range(lax.axis_size("frame")):
        for core in range(N_TENSOR):
            at = (frame - core) % PART
            target = frame // PART * PART + ((at ^ 1) + core) % PART
            pairs.append((frame * N_TENSOR + core, target * N_TENSOR + core))
    return lax.ppermute(x, ("frame", "tensor"), pairs)


def across_both(x):
    pairs = []
    for frame in range(lax.axis_size("frame")):
        for at in range(N_TENSOR):
            pairs.append((frame * N_TENSOR + at, (frame ^ PART) * N_TENSOR + (at ^ 2)))
    return lax.ppermute(x, ("frame", "tensor"), pairs)


def peer(x, mask):
    return lax.ppermute(x, "tensor", [(i, i ^ mask) for i in range(N_TENSOR)])


def shifted(x, axis, by):
    length = lax.axis_size(axis)
    pairs = [(i, i + by) for i in range(length) if 0 <= i + by < length]
    return lax.ppermute(x, axis, pairs)


def sinusoid(time_values, freq_width):
    half_width = freq_width // 2
    frequencies = jnp.exp(
        -math.log(10000.0) * jnp.arange(half_width, dtype=jnp.float32) / half_width
    )
    angles = time_values[:, None] * frequencies[None, :]
    return jnp.concatenate([jnp.cos(angles), jnp.sin(angles)], axis=-1)


def lookup(table_values, positions):
    matches = jnp.arange(table_values.shape[0], dtype=jnp.int32)[None, :] == positions[:, None]
    return jnp.sum(jnp.where(matches, table_values[None, :], 0), axis=1).astype(jnp.float32)


def dot(a, b):
    return jnp.dot(a, b, preferred_element_type=F32)


def dot_t(a, b):
    return lax.dot_general(a, b, (((1,), (1,)), ((), ())), preferred_element_type=F32)


def split3(x):
    hi = x.astype(BF16)
    rest = x - hi.astype(F32)
    mid = rest.astype(BF16)
    return hi, mid, (rest - mid.astype(F32)).astype(BF16)


def ring_heads():
    at = lax.rem(lax.axis_index("frame") - lax.rem(lax.axis_index("tensor"), 2) + PART, PART)
    pair, member = lax.div(at, 2), lax.rem(at, 2)
    ahead = lax.rem(pair + 1, SPREAD_HEADS)
    behind = lax.rem(pair + SPREAD_HEADS - 1, SPREAD_HEADS)
    first = member * ahead + (1 - member) * behind
    second = member * behind + (1 - member) * ahead
    return [pair, first, second, lax.rem(pair + 2, SPREAD_HEADS)]


def pack_kernel(q_hbm, k_hbm, v_hbm, x1_ref, x2_ref, x3_ref, kv_ref, q_out_ref, q_ref, k_ref, v_ref, sem, out_sem):
    common = pl.ds(SPREAD_HEADS * HD, HD)
    copies = [
        pltpu.make_async_copy(source, target, sem.at[at])
        for at, (source, target) in enumerate(((k_hbm, k_ref), (v_hbm, v_ref), (q_hbm, q_ref)))
    ]
    for copy in copies:
        copy.start()
    own = [pl.ds(pl.multiple_of(head * HD, HD), HD) for head in ring_heads()]
    moves = []

    def move(source, lanes, target, slot):
        moves.append(
            pltpu.make_async_copy(
                source.at[:, lanes], target.at[:, pl.ds(slot * HD, HD)], out_sem.at[len(moves)]
            )
        )
        moves[-1].start()

    targets = (kv_ref, x1_ref, x2_ref, x3_ref)
    for slot, (copy, source) in enumerate(zip(copies[:2], (k_ref, v_ref))):
        copy.wait()
        for at, ref in enumerate(targets):
            move(source, own[at], ref, slot)
        move(source, common, kv_ref, slot + 2)
    copies[2].wait()
    for at, ref in enumerate(targets[1:], 1):
        move(q_ref, own[at], ref, 2)
        move(q_ref, common, ref, 3)
    move(q_ref, own[0], q_out_ref, 0)
    move(q_ref, common, q_out_ref, 1)
    for copy in moves:
        copy.wait()


def softmax_block(query, keys, values, old=None):
    scores = [dot_t(query, key) for key in keys]
    peak = max_of([jnp.max(s, axis=1, keepdims=True) for s in scores])
    if old is not None:
        old_acc, old_peak, old_total = old
        peak = jnp.maximum(peak, old_peak)
    acc = None
    total = None
    for s, value in zip(scores, values):
        weights = jnp.exp2((s - peak) * EXP_SCALE)
        part = sum_lanes(weights)
        total = part if total is None else total + part
        mixed = dot(weights.astype(BF16), value)
        acc = mixed if acc is None else acc + mixed
    if old is not None:
        shrink = jnp.exp2((old_peak - peak) * EXP_SCALE)
        acc = acc + old_acc * shrink
        total = total + old_total * shrink
    return acc, peak, total


def attend_kernel(operand_count, last, *refs):
    refs = list(refs)
    far_q_ref, own_q_ref = refs.pop(0), refs.pop(0)
    row_count = own_q_ref.shape[0]
    far_count = far_q_ref.shape[0] // row_count
    queries = [far_q_ref[at * row_count : (at + 1) * row_count, 0:HD] for at in range(far_count)]
    queries.append(own_q_ref[:, 0:HD])
    blocks = []
    for _ in range(operand_count):
        ref = refs.pop(0)
        blocks += [(ref, low) for low in range(0, ref.shape[0], row_count)]
    states = [refs.pop(0) for _ in range(3)] if last else None
    keys = [ref[low : low + row_count, 0:HD] for ref, low in blocks]
    values = [ref[low : low + row_count, HD : 2 * HD] for ref, low in blocks]
    for at, query in enumerate(queries):
        rows = slice(at * row_count, (at + 1) * row_count)
        old = (states[0][rows, :], states[1][rows, 0:1], states[2][rows, :]) if last else None
        acc, peak, total = softmax_block(query, keys, values, old)
        if last:
            refs[at][...] = (acc / jnp.sum(total, axis=1, keepdims=True)).astype(BF16)
        else:
            refs[0][rows, :] = acc
            refs[1][rows, :] = jnp.broadcast_to(peak, acc.shape)
            refs[2][rows, :] = total


def gather_kernel(x1_ref, x2_ref, x3_ref, kv_ref, q_ref):
    row_count = x1_ref.shape[0]
    for at, ref in enumerate((x1_ref, x2_ref, x3_ref)):
        rows = slice(at * row_count, (at + 1) * row_count)
        kv_ref[rows, :] = ref[:, 0 : 2 * HD]
        q_ref[rows, :] = ref[:, 2 * HD :]


def common_kernel(own_q_ref, far_q_ref, kv0, kv1, *refs):
    row_count = own_q_ref.shape[0]
    keys = [ref[:, 2 * HD : 3 * HD] for ref in (kv0, kv1)]
    values = [ref[:, 3 * HD :] for ref in (kv0, kv1)]
    queries = [far_q_ref[at * row_count : (at + 1) * row_count, HD:] for at in range(3)]
    for at, query in enumerate((*queries, own_q_ref[:, HD:])):
        acc, peak, total = softmax_block(query, keys, values)
        total = jnp.sum(total, axis=1, keepdims=True)
        if at == 3:
            refs[3][...] = acc
            refs[4][...] = jnp.broadcast_to(peak, acc.shape)
            refs[5][...] = jnp.broadcast_to(total, acc.shape)
            continue
        refs[at][0:row_count, :] = (acc / total).astype(BF16)
        rows = []
        for value in (peak, total):
            for low in range(0, row_count, HD):
                block = jnp.broadcast_to(value[low : low + HD], (HD, HD))
                rows += [x.astype(F32) for x in split3(jnp.transpose(block)[0:1])]
        rows += [jnp.zeros((STAT_ROWS - len(rows), HD), F32)]
        refs[at][row_count:, :] = jnp.concatenate(rows, axis=0).astype(BF16)


def merge_kernel(m1, m2, m3, acc_ref, peak_ref, total_ref, own_ref, out_ref):
    out_ref[:, 0:HD] = own_ref[...]
    row_count = acc_ref.shape[0]
    stats = [ref[row_count:, :].astype(F32) for ref in (m1, m2, m3)]

    def column(stat, at):
        row = stat[3 * at : 3 * at + 1] + stat[3 * at + 1 : 3 * at + 2] + stat[3 * at + 2 : 3 * at + 3]
        return jnp.transpose(jnp.broadcast_to(row, (HD, HD)))

    count = row_count // HD
    for at in range(count):
        rows = slice(at * HD, (at + 1) * HD)
        peaks = [peak_ref[rows, :]] + [column(stat, at) for stat in stats]
        totals = [total_ref[rows, :]] + [column(stat, count + at) for stat in stats]
        top = max_of(peaks)
        shares = [jnp.exp2((peak - top) * EXP_SCALE) for peak in peaks]
        numerator = acc_ref[rows, :] * shares[0]
        denominator = totals[0] * shares[0]
        for ref, share, total in zip((m1, m2, m3), shares[1:], totals[1:]):
            weight = share * total
            numerator = numerator + ref[rows, :].astype(F32) * weight
            denominator = denominator + weight
        out_ref[rows, HD:] = (numerator / denominator).astype(BF16)


def max_of(values):
    result = values[0]
    for value in values[1:]:
        result = jnp.maximum(result, value)
    return result


def sum_lanes(x):
    result = x[:, :HD]
    for low in range(HD, x.shape[1], HD):
        result = result + x[:, low : low + HD]
    return result


def attend(far_queries, own_queries, blocks, state, cost):
    row_count = own_queries.shape[0]
    query_rows = row_count + far_queries.shape[0]
    operands = [far_queries, own_queries, *blocks] + ([] if state is None else list(state))
    if state is not None:
        out_shape = [jax.ShapeDtypeStruct((row_count, HD), BF16)] * (query_rows // row_count)
    else:
        out_shape = [jax.ShapeDtypeStruct((query_rows, HD), F32)] * 3

    def body(*refs):
        attend_kernel(len(blocks), state is not None, *refs)

    return pl.pallas_call(body, out_shape=out_shape, compiler_params=params(), cost_estimate=cost)(*operands)


def modulate_kernel(embedding_ref, time_ref, head_ref, gate_ref, lifted_ref, extra_ref):
    width = gate_ref.shape[1]
    channels = head_ref.shape[0]
    embedding = jnp.broadcast_to(embedding_ref[...], (16, TFREQ))
    gate_ref[...] = dot(embedding, time_ref[0])[:8]
    shift = dot(embedding, time_ref[1])[:1]
    lift = 1.0 + dot(embedding, time_ref[2])[:1]
    head = head_ref[...].astype(F32)
    lifted = head * lift
    high = lifted.astype(BF16)
    low = (lifted - high.astype(F32)).astype(BF16)
    lifted_ref[0:channels] = high
    lifted_ref[channels:] = low
    lift_head = jnp.sum(high.astype(F32) + low.astype(F32), axis=1, keepdims=True)
    shift_head = jnp.sum(head * shift, axis=1, keepdims=True)
    extra_ref[...] = place((lift_head, shift_head), extra_ref.shape)


def place(pieces, shape):
    lane = lax.broadcasted_iota(jnp.int32, shape, 1)
    result = jnp.zeros(shape, F32)
    for at, piece in enumerate(pieces):
        result = jnp.where(lane == at, piece.astype(F32), result)
    return result


def head_rows(head_ref, w_ref, rows, lanes):
    parts = []
    for row in rows:
        if row is None:
            parts.append(w_ref[SPREAD_HEADS * HD : (SPREAD_HEADS + 1) * HD, lanes])
        else:
            parts.append(w_ref[pl.ds(pl.multiple_of(head_ref[row] * HD, HD), HD), lanes])
    return jnp.concatenate(parts, axis=0)


def mix_kernel(out_dtype, terms, with_base, head_ref, *refs):
    refs = list(refs)
    sources = []
    for input_count, weight_count, rows, column in terms:
        inputs = [refs.pop(0) for _ in range(input_count)]
        sources.append((inputs, [refs.pop(0) for _ in range(weight_count)], rows, column))
    base_ref = refs.pop(0) if with_base else None
    out_ref = refs[0]
    width = out_ref.shape[1]
    for low in range(0, width, COLUMN_BLOCK):
        lanes = pl.ds(low, COLUMN_BLOCK)
        acc = base_ref[:, lanes] if with_base else None
        for inputs, weights, rows, column in sources:
            offset = 0 if column is None else pl.multiple_of(head_ref[column] * width, HD)
            weight = head_rows(head_ref, weights[0], rows, pl.ds(offset + low, COLUMN_BLOCK))
            value = inputs[0][...]
            if len(inputs) > 1:
                value = jnp.concatenate([ref[...] for ref in inputs], axis=1)
            part = dot(value, weight)
            acc = part if acc is None else acc + part
        out_ref[:, lanes] = acc.astype(out_dtype)


def mix(heads, width, terms, out_dtype, base=None):
    shapes, operands = [], [heads]
    for inputs, weights, rows, column in terms:
        shapes.append((len(inputs), len(weights), rows, column))
        operands += [*inputs, *weights]
    if base is not None:
        operands.append(base)
    row_count = operands[1].shape[0]

    def body(*refs):
        mix_kernel(out_dtype, shapes, base is not None, *refs)

    return pl.pallas_call(
        body,
        in_specs=[pl.BlockSpec(memory_space=pltpu.SMEM)]
        + [pl.BlockSpec(memory_space=pltpu.VMEM)] * (len(operands) - 1),
        out_shape=jax.ShapeDtypeStruct((row_count, width), out_dtype),
        compiler_params=params(),
        cost_estimate=SMALL,
    )(*operands)


def hidden_kernel(
    acc_ref, other_ref, in_ref, gate_ref, lifted_ref, extra_ref, stream_ref, message_ref
):
    row_count, width = stream_ref.shape
    channels = lifted_ref.shape[0] // 2
    total = None
    squares = None
    share = None
    rest = None
    for low in range(0, width, COLUMN_BLOCK):
        lanes = slice(low, low + COLUMN_BLOCK)
        mixed = acc_ref[:, lanes] + other_ref[:, lanes].astype(F32)
        hidden = in_ref[:, lanes].astype(F32) + gate_ref[0:1, lanes] * mixed
        high = hidden.astype(BF16)
        stream_ref[:, lanes] = high
        small = (hidden - high.astype(F32)).astype(BF16)
        parts = (
            sum_lanes(hidden),
            sum_lanes(hidden * hidden),
            dot_t(lifted_ref[:, lanes], high),
            dot_t(lifted_ref[0:channels, lanes], small),
        )
        if total is None:
            total, squares, share, rest = parts
        else:
            total, squares = total + parts[0], squares + parts[1]
            share, rest = share + parts[2], rest + parts[3]
    mean = jnp.sum(total, axis=1, keepdims=True) * (1.0 / width)
    spread = jnp.sum(squares, axis=1, keepdims=True) - mean * mean * width
    stats = jnp.transpose(place((mean, spread), (row_count, HD)))
    mean_row, spread_row = stats[0:1], stats[1:2]
    extra = extra_ref[...]
    share = share[0:channels] + share[channels:] + rest - extra[:, 0:1] * mean_row
    message_ref[0:channels, 0:row_count] = share
    message_ref[0:channels, row_count:] = extra
    message_ref[channels:, 0:row_count] = jnp.concatenate(
        [mean_row, spread_row, jnp.zeros((6, row_count), F32)], axis=0
    )
    message_ref[channels:, row_count:] = jnp.zeros((8, HD), F32)


def pair_kernel(a_ref, b_ref, out_ref):
    channels = a_ref.shape[0] - 8
    row_count = a_ref.shape[1] - HD
    width = D // N_TENSOR
    refs = (a_ref, b_ref)
    means = [ref[channels : channels + 1, 0:row_count] for ref in refs]
    spreads = [ref[channels + 1 : channels + 2, 0:row_count] for ref in refs]
    mean = (means[0] + means[1]) * 0.5
    offsets = [x - mean for x in means]
    spread = (spreads[0] + spreads[1]) + (offsets[0] * offsets[0] + offsets[1] * offsets[1]) * width
    extras = [ref[0:channels, row_count:] for ref in refs]
    shares = [ref[0:channels, 0:row_count] + o * e[:, 0:1] for ref, o, e in zip(refs, offsets, extras)]
    out_ref[0:channels, 0:row_count] = (shares[0] + shares[1]).astype(BF16)
    extra = extras[0] + extras[1]
    pieces = split3(extra[:, 0:1]) + split3(extra[:, 1:2])
    out_ref[0:channels, row_count:] = place(pieces, (channels, HD)).astype(BF16)
    rows = [x.astype(F32) for x in split3(mean) + split3(spread)]
    rows = jnp.concatenate(rows + [jnp.zeros((10, row_count), F32)], axis=0)
    out_ref[channels:, 0:row_count] = rows.astype(BF16)
    out_ref[channels:, row_count:] = jnp.zeros((16, HD), BF16)


def velocity_of(a_ref, b_ref):
    channels = a_ref.shape[0] - 16
    row_count = a_ref.shape[1] - HD
    refs = (a_ref, b_ref)
    stats = [ref[channels:, 0:row_count].astype(F32) for ref in refs]
    extras = [ref[0:channels, row_count:].astype(F32) for ref in refs]
    means = [x[0:1] + x[1:2] + x[2:3] for x in stats]
    spreads = [x[3:4] + x[4:5] + x[5:6] for x in stats]
    lifts = [x[:, 0:1] + x[:, 1:2] + x[:, 2:3] for x in extras]
    shifts = [x[:, 3:4] + x[:, 4:5] + x[:, 5:6] for x in extras]
    mean = (means[0] + means[1]) * 0.5
    offsets = [x - mean for x in means]
    variance = (spreads[0] + spreads[1]) * (1.0 / D)
    variance = variance + (offsets[0] * offsets[0] + offsets[1] * offsets[1]) * 0.5
    shares = [ref[0:channels, 0:row_count].astype(F32) + o * b for ref, o, b in zip(refs, offsets, lifts)]
    return (shares[0] + shares[1]) * lax.rsqrt(variance + 1e-06) + (shifts[0] + shifts[1])


def finish_kernel(p0, p1, latent_ref, step_ref, velocity_ref, updated_ref):
    velocity = velocity_of(p0, p1)
    velocity_ref[...] = velocity
    updated_ref[...] = (latent_ref[...] + step_ref[0, 0] * velocity).astype(BF16)


def local(
    queries,
    keys,
    values,
    stream_in,
    out_weight,
    time_weight,
    head_weight,
    latent,
    new_noise,
    levels,
    timesteps,
):
    row_count, width = stream_in.shape
    channels = latent.shape[1]
    frame_index = lax.axis_index("frame")
    frame_count = lax.axis_size("frame")
    tensor_index = lax.axis_index("tensor")
    barrier = lax.optimization_barrier

    t_now = lookup(timesteps, levels)
    t_next = lookup(timesteps, levels - 1)
    embedding = sinusoid(t_now, TFREQ).astype(BF16)
    step = ((t_next - t_now) / 1000.0).reshape(1, 1)
    head = head_weight.T
    gate, lifted, extra = pl.pallas_call(
        modulate_kernel,
        out_shape=[
            jax.ShapeDtypeStruct((8, width), F32),
            jax.ShapeDtypeStruct((2 * channels, width), BF16),
            jax.ShapeDtypeStruct((channels, HD), F32),
        ],
        compiler_params=params(),
        cost_estimate=SMALL,
    )(embedding, time_weight, head)
    tables = (gate, lifted, extra, step)

    core_index, side = tensor_index % 2, tensor_index // 2
    heads = jnp.stack(
        [
            *ring_heads(),
            side,
            core_index,
            1 - core_index,
        ]
    ).astype(jnp.int32)
    depth = out_weight.shape[0]
    kv_width, packed_width = 2 * HD, 4 * HD
    in_smem = pl.BlockSpec(memory_space=pltpu.SMEM)
    in_hbm = pl.BlockSpec(memory_space=pltpu.HBM)
    x1, x2, x3, own_kv, own_q = pl.pallas_call(
        pack_kernel,
        in_specs=[in_hbm] * 3,
        out_specs=[in_hbm] * 5,
        scratch_shapes=[pltpu.VMEM(queries.shape, BF16)] * 3
        + [pltpu.SemaphoreType.DMA((3,)), pltpu.SemaphoreType.DMA((18,))],
        out_shape=[jax.ShapeDtypeStruct((row_count, packed_width), BF16)] * 3
        + [jax.ShapeDtypeStruct((row_count, packed_width), BF16), jax.ShapeDtypeStruct((row_count, 2 * HD), BF16)],
        compiler_params=params(COPY_LIMIT),
        cost_estimate=SMALL,
    )(queries, keys, values)

    x3 = spread(x3, 3)
    x2 = spread(x2, 2)
    x1 = spread(x1, 1)
    partner = [swap_pair(own_kv)]
    partner[0], out_weight = barrier((partner[0], out_weight))
    far = [
        lax.dynamic_slice(out_weight, (0, ((1 - side) * 2 + core) * width), (depth, width))
        for core in (core_index, 1 - core_index)
    ]
    far = [peer(far[0], 2), across_both(far[1])]
    own_weight = lax.dynamic_slice(out_weight, (0, side * 2 * width), (depth, 2 * width))
    x1, x2, x3, partner, own_weight, tables, heads = barrier(
        (x1, x2, x3, partner, own_weight, tables, heads)
    )
    gate, lifted, extra, step = tables
    far_kv, far_q = pl.pallas_call(
        gather_kernel,
        out_shape=[jax.ShapeDtypeStruct((3 * row_count, kv_width), BF16)] * 2,
        compiler_params=params(),
        cost_estimate=SMALL,
    )(x1, x2, x3)
    swapped = swap_pair(far_kv)
    *parts, acc, peak, total = pl.pallas_call(
        common_kernel,
        out_shape=[jax.ShapeDtypeStruct((row_count + STAT_ROWS, HD), BF16)] * 3
        + [jax.ShapeDtypeStruct((row_count, HD), F32)] * 3,
        compiler_params=params(),
        cost_estimate=SMALL,
    )(own_q, far_q, own_kv, partner[0])
    state = attend(far_q, own_q, (own_kv, partner[0], far_kv), None, ATTEND_COST)
    parts[2], state = barrier((parts[2], state))
    parts = [spread(x, i + 1, True) for i, x in enumerate(parts)]
    *results, own_result = attend(far_q, own_q, (swapped,), state, SMALL)
    results, own_result, far = barrier((results, own_result, far))
    mine = pl.pallas_call(
        merge_kernel,
        out_shape=jax.ShapeDtypeStruct((row_count, 2 * HD), BF16),
        compiler_params=params(),
        cost_estimate=SMALL,
    )(*parts, acc, peak, total, own_result)
    back, back_across = [None] * 3, [None] * 3
    for at in (2, 1, 0):
        back[at] = spread(results[at], at + 1, True)
    for at in (0, 1, 2):
        back_across[at] = peer(back[at], 2)
    mine_across = peer(mine, 2)
    mine_rows, back_rows = (0, None), (1, 2, 3)
    sums = [
        mix(
            heads,
            width,
            [
                ([mine], [own_weight], mine_rows, column),
                (back, [own_weight], back_rows, column),
                ([mine_across], [weight], mine_rows, None),
            ],
            F32,
        )
        for column, weight in ((6, far[1]), (5, far[0]))
    ]
    sent = mix(heads, width, [(back_across, [far[1]], back_rows, None)], BF16, sums[0])
    kept = mix(heads, width, [(back_across, [far[0]], back_rows, None)], F32, sums[1])
    received = peer(sent, 1)

    stream, message = pl.pallas_call(
        hidden_kernel,
        out_shape=[
            jax.ShapeDtypeStruct((row_count, width), BF16),
            jax.ShapeDtypeStruct((channels + 8, row_count + HD), F32),
        ],
        compiler_params=params(),
        cost_estimate=SMALL,
    )(kept, received, stream_in, gate, lifted, extra)
    paired = pl.pallas_call(
        pair_kernel,
        out_shape=jax.ShapeDtypeStruct((channels + 16, row_count + HD), BF16),
        compiler_params=params(),
        cost_estimate=SMALL,
    )(message, peer(message, 1))
    velocity, updated = pl.pallas_call(
        finish_kernel,
        in_specs=[pl.BlockSpec(memory_space=pltpu.VMEM)] * 3 + [in_smem],
        out_shape=[
            jax.ShapeDtypeStruct((channels, row_count), F32),
            jax.ShapeDtypeStruct((channels, row_count), BF16),
        ],
        compiler_params=params(),
        cost_estimate=SMALL,
    )(paired, peer(paired, 2), latent.T, step)
    arrived = shifted(updated, "frame", -1).astype(F32)
    queue_next = jnp.where(frame_index == frame_count - 1, new_noise.T, arrived)
    return (stream, velocity.T, queue_next.T)


def solution(mesh):
    return jax.shard_map(
        local,
        mesh=mesh,
        in_specs=(
            P("frame", "tensor"),
            P("frame", "tensor"),
            P("frame", "tensor"),
            P("frame", "tensor"),
            P("tensor", None),
            P(None, None, "tensor"),
            P("tensor", None),
            P("frame", None),
            P(),
            P("frame"),
            P(),
        ),
        out_specs=(P("frame", "tensor"), P("frame", None), P("frame", None)),
        check_vma=False,
    )
```

```python
import math

import jax
import jax.numpy as jnp
from jax import lax
from jax.experimental import pallas as pl
from jax.experimental.pallas import tpu as pltpu
from jax.sharding import PartitionSpec as P

D = 5120
HD = 128
TFREQ = 256
PART = 8
N_TENSOR = 4
F32 = jnp.float32
BF16 = jnp.bfloat16
COLUMN_BLOCK = 256
SPREAD_HEADS = 4
STAT_ROWS = 32
SMALL = pl.CostEstimate(flops=1000, bytes_accessed=1000, transcendentals=0)
ATTEND_COST = pl.CostEstimate(flops=9_000_000_000, bytes_accessed=1000, transcendentals=0)
EXP_SCALE = HD ** (-0.5) / math.log(2.0)
VMEM_LIMIT = 16 * 1024 * 1024
COPY_LIMIT = 56 * 1024 * 1024


def params(limit=VMEM_LIMIT):
    return pltpu.CompilerParams(vmem_limit_bytes=limit)


def spread(x, distance, backward=False):
    pairs = []
    for frame in range(lax.axis_size("frame")):
        for core in range(N_TENSOR):
            at = (frame - core) % PART
            step = distance if (at + distance) % 2 == 0 else -distance
            target = frame // PART * PART + (frame + step) % PART
            pairs.append((frame * N_TENSOR + core, target * N_TENSOR + core))
    if backward:
        pairs = [(b, a) for a, b in pairs]
    return lax.ppermute(x, ("frame", "tensor"), pairs)


def swap_pair(x):
    pairs = []
    for frame in range(lax.axis_size("frame")):
        for core in range(N_TENSOR):
            at = (frame - core) % PART
            target = frame // PART * PART + ((at ^ 1) + core) % PART
            pairs.append((frame * N_TENSOR + core, target * N_TENSOR + core))
    return lax.ppermute(x, ("frame", "tensor"), pairs)


def across_both(x):
    pairs = []
    for frame in range(lax.axis_size("frame")):
        for at in range(N_TENSOR):
            pairs.append((frame * N_TENSOR + at, (frame ^ PART) * N_TENSOR + (at ^ 2)))
    return lax.ppermute(x, ("frame", "tensor"), pairs)


def peer(x, mask):
    return lax.ppermute(x, "tensor", [(i, i ^ mask) for i in range(N_TENSOR)])


def shifted(x, axis, by):
    length = lax.axis_size(axis)
    pairs = [(i, i + by) for i in range(length) if 0 <= i + by < length]
    return lax.ppermute(x, axis, pairs)


def sinusoid(time_values, freq_width):
    half_width = freq_width // 2
    frequencies = jnp.exp(
        -math.log(10000.0) * jnp.arange(half_width, dtype=jnp.float32) / half_width
    )
    angles = time_values[:, None] * frequencies[None, :]
    return jnp.concatenate([jnp.cos(angles), jnp.sin(angles)], axis=-1)


def lookup(table_values, positions):
    matches = jnp.arange(table_values.shape[0], dtype=jnp.int32)[None, :] == positions[:, None]
    return jnp.sum(jnp.where(matches, table_values[None, :], 0), axis=1).astype(jnp.float32)


def dot(a, b):
    return jnp.dot(a, b, preferred_element_type=F32)


def dot_t(a, b):
    return lax.dot_general(a, b, (((1,), (1,)), ((), ())), preferred_element_type=F32)


def split3(x):
    hi = x.astype(BF16)
    rest = x - hi.astype(F32)
    mid = rest.astype(BF16)
    return hi, mid, (rest - mid.astype(F32)).astype(BF16)


def ring_heads():
    at = lax.rem(lax.axis_index("frame") - lax.rem(lax.axis_index("tensor"), 2) + PART, PART)
    pair, member = lax.div(at, 2), lax.rem(at, 2)
    ahead = lax.rem(pair + 1, SPREAD_HEADS)
    behind = lax.rem(pair + SPREAD_HEADS - 1, SPREAD_HEADS)
    first = member * ahead + (1 - member) * behind
    second = member * behind + (1 - member) * ahead
    return [pair, first, second, lax.rem(pair + 2, SPREAD_HEADS)]


def pack_kernel(q_hbm, k_hbm, v_hbm, x1_ref, x2_ref, x3_ref, kv_ref, q_out_ref, q_ref, k_ref, v_ref, sem, out_sem):
    common = pl.ds(SPREAD_HEADS * HD, HD)
    copies = [
        pltpu.make_async_copy(source, target, sem.at[at])
        for at, (source, target) in enumerate(((k_hbm, k_ref), (v_hbm, v_ref), (q_hbm, q_ref)))
    ]
    for copy in copies:
        copy.start()
    own = [pl.ds(pl.multiple_of(head * HD, HD), HD) for head in ring_heads()]
    moves = []

    def move(source, lanes, target, slot):
        moves.append(
            pltpu.make_async_copy(
                source.at[:, lanes], target.at[:, pl.ds(slot * HD, HD)], out_sem.at[len(moves)]
            )
        )
        moves[-1].start()

    targets = (kv_ref, x1_ref, x2_ref, x3_ref)
    for slot, (copy, source) in enumerate(zip(copies[:2], (k_ref, v_ref))):
        copy.wait()
        for at, ref in enumerate(targets):
            move(source, own[at], ref, slot)
        move(source, common, kv_ref, slot + 2)
    copies[2].wait()
    for at, ref in enumerate(targets[1:], 1):
        move(q_ref, own[at], ref, 2)
        move(q_ref, common, ref, 3)
    move(q_ref, own[0], q_out_ref, 0)
    move(q_ref, common, q_out_ref, 1)
    for copy in moves:
        copy.wait()


def softmax_block(query, keys, values, old=None):
    scores = [dot_t(query, key) for key in keys]
    peak = max_of([jnp.max(s, axis=1, keepdims=True) for s in scores])
    if old is not None:
        old_acc, old_peak, old_total = old
        peak = jnp.maximum(peak, old_peak)
    acc = None
    total = None
    for s, value in zip(scores, values):
        weights = jnp.exp2((s - peak) * EXP_SCALE)
        part = sum_lanes(weights)
        total = part if total is None else total + part
        mixed = dot(weights.astype(BF16), value)
        acc = mixed if acc is None else acc + mixed
    if old is not None:
        shrink = jnp.exp2((old_peak - peak) * EXP_SCALE)
        acc = acc + old_acc * shrink
        total = total + old_total * shrink
    return acc, peak, total


def attend_kernel(operand_count, last, *refs):
    refs = list(refs)
    far_q_ref, own_q_ref = refs.pop(0), refs.pop(0)
    row_count = own_q_ref.shape[0]
    far_count = far_q_ref.shape[0] // row_count
    queries = [far_q_ref[at * row_count : (at + 1) * row_count, 0:HD] for at in range(far_count)]
    queries.append(own_q_ref[:, 0:HD])
    blocks = []
    for _ in range(operand_count):
        ref = refs.pop(0)
        blocks += [(ref, low) for low in range(0, ref.shape[0], row_count)]
    states = [refs.pop(0) for _ in range(3)] if last else None
    keys = [ref[low : low + row_count, 0:HD] for ref, low in blocks]
    values = [ref[low : low + row_count, HD : 2 * HD] for ref, low in blocks]
    for at, query in enumerate(queries):
        rows = slice(at * row_count, (at + 1) * row_count)
        old = (states[0][rows, :], states[1][rows, 0:1], states[2][rows, :]) if last else None
        acc, peak, total = softmax_block(query, keys, values, old)
        if last:
            refs[at][...] = (acc / jnp.sum(total, axis=1, keepdims=True)).astype(BF16)
        else:
            refs[0][rows, :] = acc
            refs[1][rows, :] = jnp.broadcast_to(peak, acc.shape)
            refs[2][rows, :] = total


def gather_kernel(x1_ref, x2_ref, x3_ref, kv_ref, q_ref):
    row_count = x1_ref.shape[0]
    for at, ref in enumerate((x1_ref, x2_ref, x3_ref)):
        rows = slice(at * row_count, (at + 1) * row_count)
        kv_ref[rows, :] = ref[:, 0 : 2 * HD]
        q_ref[rows, :] = ref[:, 2 * HD :]


def common_kernel(own_q_ref, far_q_ref, kv0, kv1, *refs):
    row_count = own_q_ref.shape[0]
    keys = [ref[:, 2 * HD : 3 * HD] for ref in (kv0, kv1)]
    values = [ref[:, 3 * HD :] for ref in (kv0, kv1)]
    queries = [far_q_ref[at * row_count : (at + 1) * row_count, HD:] for at in range(3)]
    for at, query in enumerate((*queries, own_q_ref[:, HD:])):
        acc, peak, total = softmax_block(query, keys, values)
        total = jnp.sum(total, axis=1, keepdims=True)
        if at == 3:
            refs[3][...] = acc
            refs[4][...] = jnp.broadcast_to(peak, acc.shape)
            refs[5][...] = jnp.broadcast_to(total, acc.shape)
            continue
        refs[at][0:row_count, :] = (acc / total).astype(BF16)
        rows = []
        for value in (peak, total):
            for low in range(0, row_count, HD):
                block = jnp.broadcast_to(value[low : low + HD], (HD, HD))
                rows += [x.astype(F32) for x in split3(jnp.transpose(block)[0:1])]
        rows += [jnp.zeros((STAT_ROWS - len(rows), HD), F32)]
        refs[at][row_count:, :] = jnp.concatenate(rows, axis=0).astype(BF16)


def merge_kernel(m1, m2, m3, acc_ref, peak_ref, total_ref, own_ref, out_ref):
    out_ref[:, 0:HD] = own_ref[...]
    row_count = acc_ref.shape[0]
    stats = [ref[row_count:, :].astype(F32) for ref in (m1, m2, m3)]

    def column(stat, at):
        row = stat[3 * at : 3 * at + 1] + stat[3 * at + 1 : 3 * at + 2] + stat[3 * at + 2 : 3 * at + 3]
        return jnp.transpose(jnp.broadcast_to(row, (HD, HD)))

    count = row_count // HD
    for at in range(count):
        rows = slice(at * HD, (at + 1) * HD)
        peaks = [peak_ref[rows, :]] + [column(stat, at) for stat in stats]
        totals = [total_ref[rows, :]] + [column(stat, count + at) for stat in stats]
        top = max_of(peaks)
        shares = [jnp.exp2((peak - top) * EXP_SCALE) for peak in peaks]
        numerator = acc_ref[rows, :] * shares[0]
        denominator = totals[0] * shares[0]
        for ref, share, total in zip((m1, m2, m3), shares[1:], totals[1:]):
            weight = share * total
            numerator = numerator + ref[rows, :].astype(F32) * weight
            denominator = denominator + weight
        out_ref[rows, HD:] = (numerator / denominator).astype(BF16)


def max_of(values):
    result = values[0]
    for value in values[1:]:
        result = jnp.maximum(result, value)
    return result


def sum_lanes(x):
    result = x[:, :HD]
    for low in range(HD, x.shape[1], HD):
        result = result + x[:, low : low + HD]
    return result


def attend(far_queries, own_queries, blocks, state, cost):
    row_count = own_queries.shape[0]
    query_rows = row_count + far_queries.shape[0]
    operands = [far_queries, own_queries, *blocks] + ([] if state is None else list(state))
    if state is not None:
        out_shape = [jax.ShapeDtypeStruct((row_count, HD), BF16)] * (query_rows // row_count)
    else:
        out_shape = [jax.ShapeDtypeStruct((query_rows, HD), F32)] * 3

    def body(*refs):
        attend_kernel(len(blocks), state is not None, *refs)

    return pl.pallas_call(body, out_shape=out_shape, compiler_params=params(), cost_estimate=cost)(*operands)


def modulate_kernel(embedding_ref, time_ref, head_ref, gate_ref, lifted_ref, extra_ref):
    width = gate_ref.shape[1]
    channels = head_ref.shape[0]
    embedding = jnp.broadcast_to(embedding_ref[...], (16, TFREQ))
    gate_ref[...] = dot(embedding, time_ref[0])[:8]
    shift = dot(embedding, time_ref[1])[:1]
    lift = 1.0 + dot(embedding, time_ref[2])[:1]
    head = head_ref[...].astype(F32)
    lifted = head * lift
    high = lifted.astype(BF16)
    low = (lifted - high.astype(F32)).astype(BF16)
    lifted_ref[0:channels] = high
    lifted_ref[channels:] = low
    lift_head = jnp.sum(high.astype(F32) + low.astype(F32), axis=1, keepdims=True)
    shift_head = jnp.sum(head * shift, axis=1, keepdims=True)
    extra_ref[...] = place((lift_head, shift_head), extra_ref.shape)


def place(pieces, shape):
    lane = lax.broadcasted_iota(jnp.int32, shape, 1)
    result = jnp.zeros(shape, F32)
    for at, piece in enumerate(pieces):
        result = jnp.where(lane == at, piece.astype(F32), result)
    return result


def head_rows(head_ref, w_ref, rows, lanes):
    parts = []
    for row in rows:
        if row is None:
            parts.append(w_ref[SPREAD_HEADS * HD : (SPREAD_HEADS + 1) * HD, lanes])
        else:
            parts.append(w_ref[pl.ds(pl.multiple_of(head_ref[row] * HD, HD), HD), lanes])
    return jnp.concatenate(parts, axis=0)


def mix_kernel(out_dtype, terms, with_base, head_ref, *refs):
    refs = list(refs)
    sources = []
    for input_count, weight_count, rows, column in terms:
        inputs = [refs.pop(0) for _ in range(input_count)]
        sources.append((inputs, [refs.pop(0) for _ in range(weight_count)], rows, column))
    base_ref = refs.pop(0) if with_base else None
    out_ref = refs[0]
    width = out_ref.shape[1]
    for low in range(0, width, COLUMN_BLOCK):
        lanes = pl.ds(low, COLUMN_BLOCK)
        acc = base_ref[:, lanes] if with_base else None
        for inputs, weights, rows, column in sources:
            offset = 0 if column is None else pl.multiple_of(head_ref[column] * width, HD)
            weight = head_rows(head_ref, weights[0], rows, pl.ds(offset + low, COLUMN_BLOCK))
            value = inputs[0][...]
            if len(inputs) > 1:
                value = jnp.concatenate([ref[...] for ref in inputs], axis=1)
            part = dot(value, weight)
            acc = part if acc is None else acc + part
        out_ref[:, lanes] = acc.astype(out_dtype)


def mix(heads, width, terms, out_dtype, base=None):
    shapes, operands = [], [heads]
    for inputs, weights, rows, column in terms:
        shapes.append((len(inputs), len(weights), rows, column))
        operands += [*inputs, *weights]
    if base is not None:
        operands.append(base)
    row_count = operands[1].shape[0]

    def body(*refs):
        mix_kernel(out_dtype, shapes, base is not None, *refs)

    return pl.pallas_call(
        body,
        in_specs=[pl.BlockSpec(memory_space=pltpu.SMEM)]
        + [pl.BlockSpec(memory_space=pltpu.VMEM)] * (len(operands) - 1),
        out_shape=jax.ShapeDtypeStruct((row_count, width), out_dtype),
        compiler_params=params(),
        cost_estimate=SMALL,
    )(*operands)


def hidden_kernel(
    acc_ref, other_ref, in_ref, gate_ref, lifted_ref, extra_ref, stream_ref, message_ref
):
    row_count, width = stream_ref.shape
    channels = lifted_ref.shape[0] // 2
    total = None
    squares = None
    share = None
    rest = None
    for low in range(0, width, COLUMN_BLOCK):
        lanes = slice(low, low + COLUMN_BLOCK)
        mixed = acc_ref[:, lanes] + other_ref[:, lanes].astype(F32)
        hidden = in_ref[:, lanes].astype(F32) + gate_ref[0:1, lanes] * mixed
        high = hidden.astype(BF16)
        stream_ref[:, lanes] = high
        small = (hidden - high.astype(F32)).astype(BF16)
        parts = (
            sum_lanes(hidden),
            sum_lanes(hidden * hidden),
            dot_t(lifted_ref[:, lanes], high),
            dot_t(lifted_ref[0:channels, lanes], small),
        )
        if total is None:
            total, squares, share, rest = parts
        else:
            total, squares = total + parts[0], squares + parts[1]
            share, rest = share + parts[2], rest + parts[3]
    mean = jnp.sum(total, axis=1, keepdims=True) * (1.0 / width)
    spread = jnp.sum(squares, axis=1, keepdims=True) - mean * mean * width
    stats = jnp.transpose(place((mean, spread), (row_count, HD)))
    mean_row, spread_row = stats[0:1], stats[1:2]
    extra = extra_ref[...]
    share = share[0:channels] + share[channels:] + rest - extra[:, 0:1] * mean_row
    message_ref[0:channels, 0:row_count] = share
    message_ref[0:channels, row_count:] = extra
    message_ref[channels:, 0:row_count] = jnp.concatenate(
        [mean_row, spread_row, jnp.zeros((6, row_count), F32)], axis=0
    )
    message_ref[channels:, row_count:] = jnp.zeros((8, HD), F32)


def pair_kernel(a_ref, b_ref, out_ref):
    channels = a_ref.shape[0] - 8
    row_count = a_ref.shape[1] - HD
    width = D // N_TENSOR
    refs = (a_ref, b_ref)
    means = [ref[channels : channels + 1, 0:row_count] for ref in refs]
    spreads = [ref[channels + 1 : channels + 2, 0:row_count] for ref in refs]
    mean = (means[0] + means[1]) * 0.5
    offsets = [x - mean for x in means]
    spread = (spreads[0] + spreads[1]) + (offsets[0] * offsets[0] + offsets[1] * offsets[1]) * width
    extras = [ref[0:channels, row_count:] for ref in refs]
    shares = [ref[0:channels, 0:row_count] + o * e[:, 0:1] for ref, o, e in zip(refs, offsets, extras)]
    out_ref[0:channels, 0:row_count] = (shares[0] + shares[1]).astype(BF16)
    extra = extras[0] + extras[1]
    pieces = split3(extra[:, 0:1]) + split3(extra[:, 1:2])
    out_ref[0:channels, row_count:] = place(pieces, (channels, HD)).astype(BF16)
    rows = [x.astype(F32) for x in split3(mean) + split3(spread)]
    rows = jnp.concatenate(rows + [jnp.zeros((10, row_count), F32)], axis=0)
    out_ref[channels:, 0:row_count] = rows.astype(BF16)
    out_ref[channels:, row_count:] = jnp.zeros((16, HD), BF16)


def velocity_of(a_ref, b_ref):
    channels = a_ref.shape[0] - 16
    row_count = a_ref.shape[1] - HD
    refs = (a_ref, b_ref)
    stats = [ref[channels:, 0:row_count].astype(F32) for ref in refs]
    extras = [ref[0:channels, row_count:].astype(F32) for ref in refs]
    means = [x[0:1] + x[1:2] + x[2:3] for x in stats]
    spreads = [x[3:4] + x[4:5] + x[5:6] for x in stats]
    lifts = [x[:, 0:1] + x[:, 1:2] + x[:, 2:3] for x in extras]
    shifts = [x[:, 3:4] + x[:, 4:5] + x[:, 5:6] for x in extras]
    mean = (means[0] + means[1]) * 0.5
    offsets = [x - mean for x in means]
    variance = (spreads[0] + spreads[1]) * (1.0 / D)
    variance = variance + (offsets[0] * offsets[0] + offsets[1] * offsets[1]) * 0.5
    shares = [ref[0:channels, 0:row_count].astype(F32) + o * b for ref, o, b in zip(refs, offsets, lifts)]
    return (shares[0] + shares[1]) * lax.rsqrt(variance + 1e-06) + (shifts[0] + shifts[1])


def finish_kernel(p0, p1, latent_ref, step_ref, velocity_ref, updated_ref):
    velocity = velocity_of(p0, p1)
    velocity_ref[...] = velocity
    updated_ref[...] = (latent_ref[...] + step_ref[0, 0] * velocity).astype(BF16)


def local(
    queries,
    keys,
    values,
    stream_in,
    out_weight,
    time_weight,
    head_weight,
    latent,
    new_noise,
    levels,
    timesteps,
):
    row_count, width = stream_in.shape
    channels = latent.shape[1]
    frame_index = lax.axis_index("frame")
    frame_count = lax.axis_size("frame")
    tensor_index = lax.axis_index("tensor")
    barrier = lax.optimization_barrier

    t_now = lookup(timesteps, levels)
    t_next = lookup(timesteps, levels - 1)
    embedding = sinusoid(t_now, TFREQ).astype(BF16)
    step = ((t_next - t_now) / 1000.0).reshape(1, 1)
    head = head_weight.T
    gate, lifted, extra = pl.pallas_call(
        modulate_kernel,
        out_shape=[
            jax.ShapeDtypeStruct((8, width), F32),
            jax.ShapeDtypeStruct((2 * channels, width), BF16),
            jax.ShapeDtypeStruct((channels, HD), F32),
        ],
        compiler_params=params(),
        cost_estimate=SMALL,
    )(embedding, time_weight, head)
    tables = (gate, lifted, extra, step)

    core_index, side = tensor_index % 2, tensor_index // 2
    heads = jnp.stack(
        [
            *ring_heads(),
            side,
            core_index,
            1 - core_index,
        ]
    ).astype(jnp.int32)
    depth = out_weight.shape[0]
    kv_width, packed_width = 2 * HD, 4 * HD
    in_smem = pl.BlockSpec(memory_space=pltpu.SMEM)
    in_hbm = pl.BlockSpec(memory_space=pltpu.HBM)
    x1, x2, x3, own_kv, own_q = pl.pallas_call(
        pack_kernel,
        in_specs=[in_hbm] * 3,
        out_specs=[in_hbm] * 5,
        scratch_shapes=[pltpu.VMEM(queries.shape, BF16)] * 3
        + [pltpu.SemaphoreType.DMA((3,)), pltpu.SemaphoreType.DMA((18,))],
        out_shape=[jax.ShapeDtypeStruct((row_count, packed_width), BF16)] * 3
        + [jax.ShapeDtypeStruct((row_count, packed_width), BF16), jax.ShapeDtypeStruct((row_count, 2 * HD), BF16)],
        compiler_params=params(COPY_LIMIT),
        cost_estimate=SMALL,
    )(queries, keys, values)

    x3 = spread(x3, 3)
    x2 = spread(x2, 2)
    x1 = spread(x1, 1)
    partner = [swap_pair(own_kv)]
    partner[0], out_weight = barrier((partner[0], out_weight))
    far = [
        lax.dynamic_slice(out_weight, (0, ((1 - side) * 2 + core) * width), (depth, width))
        for core in (core_index, 1 - core_index)
    ]
    far = [peer(far[0], 2), across_both(far[1])]
    own_weight = lax.dynamic_slice(out_weight, (0, side * 2 * width), (depth, 2 * width))
    x1, x2, x3, partner, own_weight, tables, heads = barrier(
        (x1, x2, x3, partner, own_weight, tables, heads)
    )
    gate, lifted, extra, step = tables
    far_kv, far_q = pl.pallas_call(
        gather_kernel,
        out_shape=[jax.ShapeDtypeStruct((3 * row_count, kv_width), BF16)] * 2,
        compiler_params=params(),
        cost_estimate=SMALL,
    )(x1, x2, x3)
    swapped = swap_pair(far_kv)
    *parts, acc, peak, total = pl.pallas_call(
        common_kernel,
        out_shape=[jax.ShapeDtypeStruct((row_count + STAT_ROWS, HD), BF16)] * 3
        + [jax.ShapeDtypeStruct((row_count, HD), F32)] * 3,
        compiler_params=params(),
        cost_estimate=SMALL,
    )(own_q, far_q, own_kv, partner[0])
    state = attend(far_q, own_q, (own_kv, partner[0], far_kv), None, ATTEND_COST)
    parts[2], state = barrier((parts[2], state))
    parts = [spread(x, i + 1, True) for i, x in enumerate(parts)]
    *results, own_result = attend(far_q, own_q, (swapped,), state, SMALL)
    results, own_result, far = barrier((results, own_result, far))
    mine = pl.pallas_call(
        merge_kernel,
        out_shape=jax.ShapeDtypeStruct((row_count, 2 * HD), BF16),
        compiler_params=params(),
        cost_estimate=SMALL,
    )(*parts, acc, peak, total, own_result)
    back, back_across = [None] * 3, [None] * 3
    for at in (2, 1, 0):
        back[at] = spread(results[at], at + 1, True)
    for at in (0, 1, 2):
        back_across[at] = peer(back[at], 2)
    mine_across = peer(mine, 2)
    back, back_across = [[x[at] for at in (0, 2, 1)] for x in (back, back_across)]
    mine_rows, back_rows = (0, None), (1, 3, 2)
    sums = [
        mix(
            heads,
            width,
            [
                ([mine], [own_weight], mine_rows, column),
                (back, [own_weight], back_rows, column),
            ],
            F32,
        )
        for column in (6, 5)
    ]
    sums = barrier(sums)
    sent, kept = [
        mix(
            heads,
            width,
            [(back_across, [weight], back_rows, None), ([mine_across], [weight], mine_rows, None)],
            out_dtype,
            base,
        )
        for weight, out_dtype, base in ((far[1], BF16, sums[0]), (far[0], F32, sums[1]))
    ]
    received = peer(sent, 1)

    stream, message = pl.pallas_call(
        hidden_kernel,
        out_shape=[
            jax.ShapeDtypeStruct((row_count, width), BF16),
            jax.ShapeDtypeStruct((channels + 8, row_count + HD), F32),
        ],
        compiler_params=params(),
        cost_estimate=SMALL,
    )(kept, received, stream_in, gate, lifted, extra)
    paired = pl.pallas_call(
        pair_kernel,
        out_shape=jax.ShapeDtypeStruct((channels + 16, row_count + HD), BF16),
        compiler_params=params(),
        cost_estimate=SMALL,
    )(message, peer(message, 1))
    velocity, updated = pl.pallas_call(
        finish_kernel,
        in_specs=[pl.BlockSpec(memory_space=pltpu.VMEM)] * 3 + [in_smem],
        out_shape=[
            jax.ShapeDtypeStruct((channels, row_count), F32),
            jax.ShapeDtypeStruct((channels, row_count), BF16),
        ],
        compiler_params=params(),
        cost_estimate=SMALL,
    )(paired, peer(paired, 2), latent.T, step)
    arrived = shifted(updated, "frame", -1).astype(F32)
    queue_next = jnp.where(frame_index == frame_count - 1, new_noise.T, arrived)
    return (stream, velocity.T, queue_next.T)


def solution(mesh):
    return jax.shard_map(
        local,
        mesh=mesh,
        in_specs=(
            P("frame", "tensor"),
            P("frame", "tensor"),
            P("frame", "tensor"),
            P("frame", "tensor"),
            P("tensor", None),
            P(None, None, "tensor"),
            P("tensor", None),
            P("frame", None),
            P(),
            P("frame"),
            P(),
        ),
        out_specs=(P("frame", "tensor"), P("frame", None), P("frame", None)),
        check_vma=False,
    )
```
